256 devices in a mesh: row: 16 (over z_hi, x, core), col: 16 (over y, z_lo).
Axes of the slice: x: 4, y: 4, z: 8 (z_hi: 2, z_lo: 4; z = z_hi * 4 + z_lo), core: 2. Of those that a mesh axis runs over, the one named last changes fastest.
Arguments:
- eigvec: float32 [28672, 8192], P('row', 'col'), may hold values from -6 to 6
- householder: float32 [4, 28672, 256], P(None, 'row', 'col'), may hold values from -0.03125 to 0.03125
- panel_factors: float32 [4, 2, 128, 128], replicated, may hold values from -1 to 1.5, as said below
Outputs:
- transformed: float32 [28672, 8192], P('row', 'col')
The draws below stay inside these ranges and needn't reach their ends.
Inputs may be any that keep to these rules, and one draw needn't show every extreme that they name: Each panel_factors[b, i] is upper triangular.
All inputs are finite; a program needn't handle non-finite values.
Results may differ from the reference program's by a relative error of at most 0.0001.
Values sent between devices are 32-bit elements; how exact they have to be, the bound alone decides.
A program may use at most 64 MiB of HBM per device.

```python
import math
import jax
import jax.numpy as jnp
from jax import lax

P_SIZE = 128
K = 256
M = 28672
NE = 8192
BLOCKS = 4


def draw_panel_factors(key, part):
    key = jax.random.fold_in(key, 7)
    diag_key, above_key = jax.random.split(key)
    diagonal = jax.random.uniform(diag_key, (BLOCKS, 2, P_SIZE), jnp.float32, 0.5, 1.5)
    above = jnp.clip(jax.random.normal(above_key, (BLOCKS, 2, P_SIZE, P_SIZE), jnp.float32), -4.0, 4.0) * (0.4 / math.sqrt(P_SIZE))
    triangle = jnp.triu(above, 1) + diagonal[..., None] * jnp.eye(P_SIZE, dtype=jnp.float32)
    return triangle


def block_scale(own_key, extent, shards, low, top_value):
    gain = 1.0
    for axis_at, shards_of in shards:
        heights = jax.random.uniform(jax.random.fold_in(jax.random.fold_in(own_key, 6), axis_at), (shards_of,), jnp.float32, low / len(shards), top_value / len(shards))
        gain = gain * jnp.repeat(jnp.exp(heights), extent[axis_at] // shards_of).reshape((-1,) + (1,) * (len(extent) - 1 - axis_at))
    return gain


def scatter_about(stream_key, extent, width, reach, cuts=(), kind=jnp.bfloat16):
    drawn = jax.random.normal(stream_key, extent, jnp.float32) * width
    if len(cuts) > 0:
        drawn = block_scale(stream_key, extent, cuts, -0.22, 0.18) * drawn
    return jnp.clip(drawn, min=-reach, max=reach).astype(kind)


def setup_inputs(seed: int = 0) -> dict:
    seeds = jax.random.split(jax.random.key(seed), 4)
    eigvec = scatter_about(seeds[0], (M, NE), 1.0, 6.0, ((0, 16), (1, 16)), jnp.float32)
    householder = scatter_about(seeds[1], (BLOCKS, M, K), M ** -0.5, 0.03125, ((1, 16), (2, 16)), jnp.float32)
    panel_factors = draw_panel_factors(jax.random.fold_in(seeds[3], 71), 0)
    return dict(eigvec=eigvec, householder=householder, panel_factors=panel_factors)


def precise_dot(left, right):
    return jnp.dot(left, right, precision=lax.Precision.HIGHEST, preferred_element_type=jnp.float32)


def reference(eigvec, householder, panel_factors):
    vectors = eigvec
    for window in range(BLOCKS):
        reflectors = householder[window]
        lead_panel = reflectors[:, :P_SIZE]
        tail_panel = reflectors[:, P_SIZE:]
        lead_factor = panel_factors[window, 0]
        tail_factor = panel_factors[window, 1]
        coupling = precise_dot(lead_panel.T, tail_panel)
        corner = -precise_dot(precise_dot(lead_factor, coupling), tail_factor)
        upper_rows = jnp.concatenate([lead_factor, corner], axis=1)
        lower_rows = jnp.concatenate([jnp.zeros((P_SIZE, P_SIZE), jnp.float32), tail_factor], axis=1)
        joined_factor = jnp.concatenate([upper_rows, lower_rows], axis=0)
        projection = precise_dot(reflectors.T, vectors)
        scaled = precise_dot(joined_factor, projection)
        vectors = vectors - precise_dot(reflectors, scaled)
    return vectors
```

```python
import functools
import jax
import jax.numpy as jnp
from jax import lax
from jax.experimental import pallas as pl
from jax.experimental.pallas import tpu as pltpu
from jax.sharding import PartitionSpec as P

MESH = pl.DeviceIdType.MESH
F32 = jnp.float32
BF16 = jnp.bfloat16
NT = (((1,), (1,)), ((), ()))
NN = (((1,), (0,)), ((), ()))
BLOCKS = 4
K = 256
PANEL = 128
ROWS = 1792
COLS = 512
HALF = COLS // 2
PIECE = HALF // 4
OWN = 16
RUN = 4 * OWN
C_HALF = PANEL // 2


def split(value):
    high = value.astype(BF16)
    low = (value - high.astype(F32)).astype(BF16)
    return high, low


def dot(a, b, dims):
    return lax.dot_general(a, b, dims, preferred_element_type=F32)


def dot3(a_high, a_low, b_high, b_low, dims):
    small = dot(a_low, b_high, dims) + dot(a_high, b_low, dims)
    return dot(a_high, b_high, dims) + small


def exact(a, b, dims):
    return lax.dot_general(
        a, b, dims, precision=lax.Precision.HIGHEST, preferred_element_type=F32
    )


def kernel(
    z_ref, w_ref, t_ref, out_ref,
    zs, zt, zh, zl, wt, wh, wl, tf,
    pt, rc, rx, ps, rz, cp, cc, cx, cs, cz, cf, st,
    local_sem, zg_s, zg_r, yg_s, yg_r, fg_s, fg_r,
    pc_s, pc_r, px_s, px_r, pz_s, pz_r,
    cc_s, cc_r, cx_s, cx_r, cz_s, cz_r, cf_s, cf_r,
    sx_s, sx_r, sc_s, sc_r,
):
    row, col = lax.axis_index("row"), lax.axis_index("col")
    z_hi, x, core = row // 8, (row // 2) % 4, row % 2
    y, z_lo = col // 4, col % 4

    def at_row(hi, xx, cc_):
        return (hi * 8 + xx * 2 + cc_, col)

    def at_col(yy, zz):
        return (row, yy * 4 + zz)

    sibling = at_row(z_hi, x, 1 - core)
    across = at_row(1 - z_hi, x, core)
    x_peers = [at_row(z_hi, (x + d) % 4, core) for d in (1, 2, 3)]
    z_peers = [at_col(y, (z_lo + d) % 4) for d in (1, 2, 3)]
    y_up, y_down = (y + 1) % 4, (y + 3) % 4
    y_peers = [at_col(y_up, z_lo), at_col(y_down, z_lo)]

    own_rows = pl.ds(pl.multiple_of(col * OWN, OWN), OWN)
    run_rows = pl.ds(pl.multiple_of(y * RUN, RUN), RUN)
    first_half = pl.ds(pl.multiple_of(y_down * RUN, RUN), RUN // 2)
    last_half = pl.ds(pl.multiple_of(y_up * RUN + RUN // 2, RUN // 2), RUN // 2)
    mine = pl.multiple_of(core * HALF, HALF)
    theirs = pl.multiple_of((1 - core) * HALF, HALF)
    piece_rows = pl.ds(pl.multiple_of(mine + x * PIECE, PIECE), PIECE)
    c_mine = pl.ds(pl.multiple_of(core * C_HALF, C_HALF), C_HALF)
    c_theirs = pl.ds(pl.multiple_of((1 - core) * C_HALF, C_HALF), C_HALF)

    sent = []

    def send(src, dst, send_sem, recv_sem, device):
        copy = pltpu.make_async_remote_copy(
            src_ref=src, dst_ref=dst, send_sem=send_sem, recv_sem=recv_sem,
            device_id=device, device_id_type=MESH,
        )
        copy.start()
        sent.append(copy)
        return copy

    fetch_z = pltpu.make_async_copy(z_ref, zs, local_sem.at[0])
    fetch_z.start()
    fetch_t = pltpu.make_async_copy(t_ref, tf, local_sem.at[1])
    fetch_t.start()
    fetch_w = []
    for b in range(BLOCKS):
        copy = pltpu.make_async_copy(w_ref.at[b], wt.at[b, own_rows], local_sem.at[2 + b])
        copy.start()
        fetch_w.append(copy)

    barrier = pltpu.get_barrier_semaphore()
    peers = [sibling, across] + x_peers + z_peers + y_peers
    for peer in peers:
        pl.semaphore_signal(barrier, inc=1, device_id=peer, device_id_type=MESH)
    pl.semaphore_wait(barrier, len(peers))

    gather_z, gather_y, gather_f = {}, {}, {}

    def z_send(b):
        gather_z[b] = [
            send(w_ref.at[b], wt.at[b, own_rows], zg_s.at[b, d], zg_r.at[b, d], z_peers[d])
            for d in range(3)
        ]

    def y_send(b):
        fetch_w[b].wait()
        for copy in gather_z[b]:
            copy.wait_recv()
        run = wt.at[b, run_rows]
        gather_y[b] = [
            send(run, run, yg_s.at[b, d], yg_r.at[b, d], y_peers[d]) for d in range(2)
        ]

    def f_send(b):
        up, down = gather_y[b]
        up.wait_recv()
        part = wt.at[b, first_half]
        one = send(part, part, fg_s.at[b, 0], fg_r.at[b, 0], y_peers[0])
        down.wait_recv()
        part = wt.at[b, last_half]
        two = send(part, part, fg_s.at[b, 1], fg_r.at[b, 1], y_peers[1])
        gather_f[b] = [one, two]

    def arrive(b):
        for copy in gather_f[b]:
            copy.wait_recv()

    z_send(0)

    fetch_z.wait()

    @pl.loop(0, ROWS // 128)
    def _(i):
        at = pl.ds(pl.multiple_of(i * 128, 128), 128)
        turned = zs[at, :].T
        zt[:, at] = turned
        zh[:, at], zl[:, at] = split(turned)

    y_send(0)
    z_send(1)
    f_send(0)
    fetch_t.wait()

    def project(b, start):
        at = pl.ds(start, HALF)
        pt[b, at, :] = dot3(zh[at, :], zl[at, :], wh[...], wl[...], NT)

    def update(b, start):
        at = pl.ds(start, HALF)
        s_high, s_low = split(st[b, at, :])

        @pl.loop(0, ROWS // K)
        def _(i):
            lanes = pl.ds(pl.multiple_of(i * K, K), K)
            fresh = zt[at, lanes] - dot3(s_high, s_low, wh[:, lanes], wl[:, lanes], NN)
            zt[at, lanes] = fresh
            zh[at, lanes], zl[at, lanes] = split(fresh)

    for b in range(BLOCKS):
        arrive(b)

        @pl.loop(0, ROWS // K)
        def _(i):
            lanes = pl.ds(pl.multiple_of(i * K, K), K)
            wh[:, lanes], wl[:, lanes] = split(wt[b, :, lanes])

        cp[b] = dot3(wh[PANEL:, :], wl[PANEL:, :], wh[:PANEL, :], wl[:PANEL, :], NT)
        c_core = send(cp.at[b, c_theirs], cc.at[b], cc_s.at[b], cc_r.at[b], sibling)
        project(b, theirs)
        p_core = send(
            pt.at[b, pl.ds(theirs, HALF)], rc.at[b], pc_s.at[b], pc_r.at[b], sibling
        )
        c_core.wait_recv()
        cp[b, c_mine, :] = cp[b, c_mine, :] + cc[b]
        c_x = [
            send(cp.at[b, c_mine], cx.at[b, d], cx_s.at[b, d], cx_r.at[b, d], x_peers[d])
            for d in range(3)
        ]
        project(b, mine)
        p_core.wait_recv()
        at = pl.ds(mine, HALF)
        pt[b, at, :] = pt[b, at, :] + rc[b]
        p_x = []
        for d in range(3):
            to = pl.multiple_of(mine + ((x + 1 + d) % 4) * PIECE, PIECE)
            p_x.append(
                send(
                    pt.at[b, pl.ds(to, PIECE)], rx.at[b, d],
                    px_s.at[b, d], px_r.at[b, d], x_peers[d],
                )
            )
        if b + 1 < BLOCKS:
            y_send(b + 1)
        if b + 2 < BLOCKS:
            z_send(b + 2)
        for copy in c_x:
            copy.wait_recv()
        cs[b] = (cp[b, c_mine, :] + cx[b, 0]) + (cx[b, 1] + cx[b, 2])
        c_z = send(cs.at[b], cz.at[b], cz_s.at[b], cz_r.at[b], across)
        for copy in p_x:
            copy.wait_recv()
        ps[b] = (pt[b, piece_rows, :] + rx[b, 0]) + (rx[b, 1] + rx[b, 2])
        p_z = send(ps.at[b], rz.at[b], pz_s.at[b], pz_r.at[b], across)
        c_z.wait_recv()
        cf[b, c_mine, :] = cs[b] + cz[b]
        c_f = send(cf.at[b, c_mine], cf.at[b, c_mine], cf_s.at[b], cf_r.at[b], sibling)
        if b + 1 < BLOCKS:
            f_send(b + 1)
        p_z.wait_recv()
        total = ps[b] + rz[b]
        tail = exact(total[:, PANEL:], tf[b, 1], NT)
        c_f.wait_recv()
        lead = exact(total[:, :PANEL] - exact(tail, cf[b], NN), tf[b, 0], NT)
        st[b, piece_rows, :PANEL] = lead
        st[b, piece_rows, PANEL:] = tail
        s_x = [
            send(
                st.at[b, piece_rows], st.at[b, piece_rows],
                sx_s.at[b, d], sx_r.at[b, d], x_peers[d],
            )
            for d in range(3)
        ]
        for copy in s_x:
            copy.wait_recv()
        part = st.at[b, pl.ds(mine, HALF)]
        s_core = send(part, part, sc_s.at[b], sc_r.at[b], sibling)
        update(b, mine)
        s_core.wait_recv()
        update(b, theirs)

    store = pltpu.make_async_copy(zt, out_ref, local_sem.at[0])
    store.start()
    for copy in sent:
        copy.wait_send()
    store.wait()


def per_device(eigvec, householder, panel_factors):
    dma = pltpu.SemaphoreType.DMA
    n = BLOCKS
    scratch = [
        pltpu.VMEM((ROWS, COLS), F32),
        pltpu.VMEM((COLS, ROWS), F32),
        pltpu.VMEM((COLS, ROWS), BF16),
        pltpu.VMEM((COLS, ROWS), BF16),
        pltpu.VMEM((n, K, ROWS), F32),
        pltpu.VMEM((K, ROWS), BF16),
        pltpu.VMEM((K, ROWS), BF16),
        pltpu.VMEM((n, 2, PANEL, PANEL), F32),
        pltpu.VMEM((n, COLS, K), F32),
        pltpu.VMEM((n, HALF, K), F32),
        pltpu.VMEM((n, 3, PIECE, K), F32),
        pltpu.VMEM((n, PIECE, K), F32),
        pltpu.VMEM((n, PIECE, K), F32),
        pltpu.VMEM((n, PANEL, PANEL), F32),
        pltpu.VMEM((n, C_HALF, PANEL), F32),
        pltpu.VMEM((n, 3, C_HALF, PANEL), F32),
        pltpu.VMEM((n, C_HALF, PANEL), F32),
        pltpu.VMEM((n, C_HALF, PANEL), F32),
        pltpu.VMEM((n, PANEL, PANEL), F32),
        pltpu.VMEM((n, COLS, K), F32),
        dma((2 + n,)),
        dma((n, 3)), dma((n, 3)), dma((n, 2)), dma((n, 2)), dma((n, 2)), dma((n, 2)),
        dma((n,)), dma((n,)), dma((n, 3)), dma((n, 3)), dma((n,)), dma((n,)),
        dma((n,)), dma((n,)), dma((n, 3)), dma((n, 3)), dma((n,)), dma((n,)), dma((n,)), dma((n,)),
        dma((n, 3)), dma((n, 3)), dma((n,)), dma((n,)),
    ]
    turned = pl.pallas_call(
        kernel,
        out_shape=jax.ShapeDtypeStruct((COLS, ROWS), F32),
        in_specs=[pl.BlockSpec(memory_space=pl.ANY)] * 3,
        out_specs=pl.BlockSpec(memory_space=pl.ANY),
        scratch_shapes=scratch,
        compiler_params=pltpu.CompilerParams(
            collective_id=0, has_side_effects=True, vmem_limit_bytes=56 << 20
        ),
        cost_estimate=pl.CostEstimate(
            flops=2 * 2 * 3 * n * K * ROWS * COLS, bytes_accessed=8 << 20, transcendentals=0
        ),
        name="back_transform",
    )(eigvec, jnp.transpose(householder, (0, 2, 1)), panel_factors)
    return turned.T


def solution(mesh):
    in_specs = (P("row", "col"), P(None, "row", "col"), P())
    out_specs = P("row", "col")
    return jax.shard_map(
        per_device, mesh=mesh, in_specs=in_specs, out_specs=out_specs, check_vma=False
    )
```

```python
import functools
import jax
import jax.numpy as jnp
from jax import lax
from jax.experimental import pallas as pl
from jax.experimental.pallas import tpu as pltpu
from jax.sharding import PartitionSpec as P

MESH = pl.DeviceIdType.MESH
F32 = jnp.float32
BF16 = jnp.bfloat16
NT = (((1,), (1,)), ((), ()))
NN = (((1,), (0,)), ((), ()))
BLOCKS = 4
K = 256
PANEL = 128
ROWS = 1792
COLS = 512
HALF = COLS // 2
PIECE = HALF // 4
UNITS = 2 * BLOCKS
RUN = 64
WIDE = (BLOCKS - 1) * K
C_HALF = PANEL // 2
ORDER = (
    "z0", "z1", "t0", "y0", "z2", "y1", "z3", "y0", "y2", "z4", "y1", "y3", "z5", "y0", "y2",
    "y4", "z6", "y1", "g1", "c0", "p0", "g1", "c0", "p0", "y3", "y5", "z7", "g1", "y2", "c0",
    "p0", "y4", "y6", "g1", "y3", "g2", "c1", "c0", "p1", "g2", "y5", "y7", "c0", "p0", "s0",
    "p1", "c1", "y4", "g2", "s0", "y6", "g1", "g2", "s0", "y5", "g3", "p1", "c2", "c1", "p2",
    "y7", "g3", "c2", "p2", "y6", "g1", "g2", "g3", "y7", "g2", "c3", "c2", "c1", "p3", "p2",
    "c3", "p3", "g3", "g1", "g1", "c1", "p1", "s1", "g3", "c2", "g2", "c3", "g2", "g3", "c2",
    "p2", "s2", "p3", "s1", "c3", "s1", "g3", "g3", "c3", "p3", "s3", "s2", "s2", "s3", "s3",
)


def split(value):
    high = value.astype(BF16)
    low = (value - high.astype(F32)).astype(BF16)
    return high, low


def dot(a, b, dims):
    return lax.dot_general(a, b, dims, preferred_element_type=F32)


def dot3(a_high, a_low, b_high, b_low, dims):
    small = dot(a_low, b_high, dims) + dot(a_high, b_low, dims)
    return dot(a_high, b_high, dims) + small


def exact(a, b, dims):
    return lax.dot_general(
        a, b, dims, precision=lax.Precision.HIGHEST, preferred_element_type=F32
    )


def kernel(
    z_ref, w_ref, t_ref, out_ref,
    zs, zt, zh, zl, wt, wh, wl, tf,
    pt, rc, rx, ps, rz, cp, cc, cx, cs, cz, cf, gp, gc, gx, gs, gz, gt, fix, st,
    local_sem, zg_s, zg_r, yg_s, yg_r, fg_s, fg_r,
    pc_s, pc_r, px_s, px_r, pz_s, pz_r,
    cc_s, cc_r, cx_s, cx_r, cz_s, cz_r, cf_s, cf_r,
    gc_s, gc_r, gx_s, gx_r, gz_s, gz_r, gy_s, gy_r, gf_s, gf_r, ga_s, ga_r, ge_s, ge_r,
    sx_s, sx_r, sc_s, sc_r,
):
    row, col = lax.axis_index("row"), lax.axis_index("col")
    z_hi, x, core = row // 8, (row // 2) % 4, row % 2
    y, z_lo = col // 4, col % 4

    def at_row(hi, xx, cc_):
        return (hi * 8 + xx * 2 + cc_, col)

    def at_col(yy, zz):
        return (row, yy * 4 + zz)

    sibling = at_row(z_hi, x, 1 - core)
    across = at_row(1 - z_hi, x, core)
    x_peers = [at_row(z_hi, (x + d) % 4, core) for d in (1, 2, 3)]
    z_peers = [at_col(y, (z_lo + d) % 4) for d in (1, 2, 3)]
    y_up, y_down = (y + 1) % 4, (y + 3) % 4
    y_peers = [at_col(y_up, z_lo), at_col(y_down, z_lo)]

    mine = pl.multiple_of(core * HALF, HALF)
    theirs = pl.multiple_of((1 - core) * HALF, HALF)
    piece_rows = pl.ds(pl.multiple_of(mine + x * PIECE, PIECE), PIECE)
    c_mine = pl.ds(pl.multiple_of(core * C_HALF, C_HALF), C_HALF)
    c_theirs = pl.ds(pl.multiple_of((1 - core) * C_HALF, C_HALF), C_HALF)

    sent = []

    def send(src, dst, send_sem, recv_sem, device):
        copy = pltpu.make_async_remote_copy(
            src_ref=src, dst_ref=dst, send_sem=send_sem, recv_sem=recv_sem,
            device_id=device, device_id_type=MESH,
        )
        copy.start()
        sent.append(copy)
        return copy

    def received(copies):
        for copy in copies:
            copy.wait_recv()

    fetch_w = []
    for b in range(BLOCKS):
        copy = pltpu.make_async_copy(w_ref.at[b], wt.at[b, col], local_sem.at[2 + b])
        copy.start()
        fetch_w.append(copy)
    fetch_z = pltpu.make_async_copy(z_ref, zs, local_sem.at[0])
    fetch_z.start()
    fetch_t = pltpu.make_async_copy(t_ref, tf, local_sem.at[1])
    fetch_t.start()

    barrier = pltpu.get_barrier_semaphore()
    peers = [sibling, across] + x_peers + z_peers + y_peers
    for peer in peers:
        pl.semaphore_signal(barrier, inc=1, device_id=peer, device_id_type=MESH)
    pl.semaphore_wait(barrier, len(peers))

    def weights(b):
        @pl.loop(0, ROWS // K)
        def _(i):
            lanes = pl.ds(pl.multiple_of(i * K, K), K)
            both = wt[b, :, :, :, lanes].reshape(K, K)
            wh[b, :, lanes], wl[b, :, lanes] = split(both)

    def project(b, start):
        at = pl.ds(start, HALF)
        pt[b, at, :] = dot3(zh[at, :], zl[at, :], wh[b], wl[b], NT)

    def update(b, start):
        at = pl.ds(start, HALF)
        s_high, s_low = split(st[b, at, :])

        @pl.loop(0, ROWS // K)
        def _(i):
            lanes = pl.ds(pl.multiple_of(i * K, K), K)
            zt[at, lanes] -= dot3(s_high, s_low, wh[b, :, lanes], wl[b, :, lanes], NN)

    gathered = [None] * UNITS

    def z_flow(u):
        b, h = u // 2, u % 2
        gathered[u] = [
            send(w_ref.at[b, h], wt.at[b, col, h], zg_s.at[u, d], zg_r.at[u, d], z_peers[d])
            for d in range(3)
        ]
        yield

    def y_flow(u):
        b, h = u // 2, u % 2
        if h == 0:
            fetch_w[b].wait()
        received(gathered[u])
        run = wt.at[b, pl.ds(4 * y, 4), h]
        up, down = [
            send(run, run, yg_s.at[u, d], yg_r.at[u, d], y_peers[d]) for d in range(2)
        ]
        yield
        up.wait_recv()
        part = wt.at[b, pl.ds(4 * y_down, 2), h]
        one = send(part, part, fg_s.at[u, 0], fg_r.at[u, 0], y_peers[0])
        down.wait_recv()
        part = wt.at[b, pl.ds(4 * y_up + 2, 2), h]
        two = send(part, part, fg_s.at[u, 1], fg_r.at[u, 1], y_peers[1])
        yield
        received([one, two])
        if h == 1:
            weights(b)
        yield

    def c_flow(b):
        cp[b] = dot3(wh[b, PANEL:, :], wl[b, PANEL:, :], wh[b, :PANEL, :], wl[b, :PANEL, :], NT)
        to_core = send(cp.at[b, c_theirs], cc.at[b], cc_s.at[b], cc_r.at[b], sibling)
        yield
        to_core.wait_recv()
        cp[b, c_mine, :] = cp[b, c_mine, :] + cc[b]
        to_x = [
            send(cp.at[b, c_mine], cx.at[b, d], cx_s.at[b, d], cx_r.at[b, d], x_peers[d])
            for d in range(3)
        ]
        yield
        received(to_x)
        cs[b] = (cp[b, c_mine, :] + cx[b, 0]) + (cx[b, 1] + cx[b, 2])
        to_z = send(cs.at[b], cz.at[b], cz_s.at[b], cz_r.at[b], across)
        yield
        to_z.wait_recv()
        cf[b, c_mine, :] = cs[b] + cz[b]
        part = cf.at[b, c_mine]
        to_core = send(part, part, cf_s.at[b], cf_r.at[b], sibling)
        yield
        to_core.wait_recv()
        yield

    def p_flow(b):
        project(b, theirs)
        to_core = send(
            pt.at[b, pl.ds(theirs, HALF)], rc.at[b], pc_s.at[b], pc_r.at[b], sibling
        )
        project(b, mine)
        yield
        to_core.wait_recv()
        at = pl.ds(mine, HALF)
        pt[b, at, :] = pt[b, at, :] + rc[b]
        to_x = []
        for d in range(3):
            to = pl.multiple_of(mine + ((x + 1 + d) % 4) * PIECE, PIECE)
            to_x.append(
                send(
                    pt.at[b, pl.ds(to, PIECE)], rx.at[b, d],
                    px_s.at[b, d], px_r.at[b, d], x_peers[d],
                )
            )
        yield
        received(to_x)
        ps[b] = (pt[b, piece_rows, :] + rx[b, 0]) + (rx[b, 1] + rx[b, 2])
        to_z = send(ps.at[b], rz.at[b], pz_s.at[b], pz_r.at[b], across)
        yield
        to_z.wait_recv()
        yield

    def g_flow(b):
        g, wide = b - 1, b * K
        own = wt[b, pl.ds(4 * y, 4)].reshape(RUN, ROWS)
        own_high, own_low = split(own)
        for c in range(b):
            gp[g, :, c * K : (c + 1) * K] = dot3(own_high, own_low, wh[c], wl[c], NT)
        lanes = pl.ds(0, wide)
        base = pl.multiple_of(core * 32, 32)
        other = pl.multiple_of((1 - core) * 32, 32)
        to_core = send(
            gp.at[g, pl.ds(other, 32), lanes], gc.at[g, :, lanes], gc_s.at[g], gc_r.at[g], sibling
        )
        yield
        to_core.wait_recv()
        at = pl.ds(base, 32)
        gp[g, at, :wide] = gp[g, at, :wide] + gc[g, :, :wide]
        to_x = []
        for d in range(3):
            to = pl.multiple_of(base + ((x + 1 + d) % 4) * 8, 8)
            to_x.append(
                send(
                    gp.at[g, pl.ds(to, 8), lanes], gx.at[g, d, :, lanes],
                    gx_s.at[g, d], gx_r.at[g, d], x_peers[d],
                )
            )
        yield
        received(to_x)
        at = pl.ds(pl.multiple_of(base + x * 8, 8), 8)
        gs[g, :, :wide] = (gp[g, at, :wide] + gx[g, 0, :, :wide]) + (
            gx[g, 1, :, :wide] + gx[g, 2, :, :wide]
        )
        to_z = send(
            gs.at[g, :, lanes], gz.at[g, :, lanes], gz_s.at[g], gz_r.at[g], across
        )
        yield
        to_z.wait_recv()
        gt[g, y, core, x, :, :wide] = gs[g, :, :wide] + gz[g, :, :wide]
        part = gt.at[g, y, core, x, :, lanes]
        up, down = [
            send(part, part, gy_s.at[g, d], gy_r.at[g, d], y_peers[d]) for d in range(2)
        ]
        yield
        up.wait_recv()
        part = gt.at[g, y_down, core, x, :, pl.ds(0, wide // 2)]
        one = send(part, part, gf_s.at[g, 0], gf_r.at[g, 0], y_peers[0])
        down.wait_recv()
        part = gt.at[g, y_up, core, x, :, pl.ds(wide // 2, wide // 2)]
        two = send(part, part, gf_s.at[g, 1], gf_r.at[g, 1], y_peers[1])
        yield
        received([one, two])
        part = gt.at[g, :, core, x, :, lanes]
        to_x = [
            send(part, part, ga_s.at[g, d], ga_r.at[g, d], x_peers[d]) for d in range(3)
        ]
        yield
        received(to_x)
        part = gt.at[g, :, core, :, :, lanes]
        to_core = send(part, part, ge_s.at[g], ge_r.at[g], sibling)
        yield
        to_core.wait_recv()
        total = None
        for c in range(b):
            seen = gt[g, :, :, :, :, c * K : (c + 1) * K].reshape(K, K)
            term = exact(st[c, piece_rows, :], seen, NT)
            total = term if total is None else total + term
        fix[g] = total
        yield

    def s_flow(b):
        total = ps[b] + rz[b]
        if b:
            total = total - fix[b - 1]
        tail = exact(total[:, PANEL:], tf[b, 1], NT)
        lead = exact(total[:, :PANEL] - exact(tail, cf[b], NN), tf[b, 0], NT)
        st[b, piece_rows, :PANEL] = lead
        st[b, piece_rows, PANEL:] = tail
        part = st.at[b, piece_rows]
        to_x = [
            send(part, part, sx_s.at[b, d], sx_r.at[b, d], x_peers[d]) for d in range(3)
        ]
        yield
        received(to_x)
        part = st.at[b, pl.ds(mine, HALF)]
        to_core = send(part, part, sc_s.at[b], sc_r.at[b], sibling)
        if b == BLOCKS - 1:
            update(b, mine)
        yield
        to_core.wait_recv()
        if b < BLOCKS - 1:
            update(b, mine)
        update(b, theirs)
        yield

    def start(_):
        fetch_t.wait()
        fetch_z.wait()

        @pl.loop(0, ROWS // 128)
        def _(i):
            at = pl.ds(pl.multiple_of(i * 128, 128), 128)
            turned = zs[at, :].T
            zt[:, at] = turned
            zh[:, at], zl[:, at] = split(turned)

        yield

    flows = {"t": start, "z": z_flow, "y": y_flow, "c": c_flow, "p": p_flow, "g": g_flow, "s": s_flow}
    steps = {}
    for name in ORDER:
        if name not in steps:
            steps[name] = flows[name[0]](int(name[1:]))
        next(steps[name])

    store = pltpu.make_async_copy(zt, out_ref, local_sem.at[0])
    store.start()
    for copy in sent:
        copy.wait_send()
    store.wait()


def per_device(eigvec, householder, panel_factors):
    dma = pltpu.SemaphoreType.DMA
    n, g = BLOCKS, BLOCKS - 1
    scratch = [
        pltpu.VMEM((ROWS, COLS), F32),
        pltpu.VMEM((COLS, ROWS), F32),
        pltpu.VMEM((COLS, ROWS), BF16),
        pltpu.VMEM((COLS, ROWS), BF16),
        pltpu.VMEM((n, 16, 2, 8, ROWS), F32),
        pltpu.VMEM((n, K, ROWS), BF16),
        pltpu.VMEM((n, K, ROWS), BF16),
        pltpu.VMEM((n, 2, PANEL, PANEL), F32),
        pltpu.VMEM((n, COLS, K), F32),
        pltpu.VMEM((n, HALF, K), F32),
        pltpu.VMEM((n, 3, PIECE, K), F32),
        pltpu.VMEM((n, PIECE, K), F32),
        pltpu.VMEM((n, PIECE, K), F32),
        pltpu.VMEM((n, PANEL, PANEL), F32),
        pltpu.VMEM((n, C_HALF, PANEL), F32),
        pltpu.VMEM((n, 3, C_HALF, PANEL), F32),
        pltpu.VMEM((n, C_HALF, PANEL), F32),
        pltpu.VMEM((n, C_HALF, PANEL), F32),
        pltpu.VMEM((n, PANEL, PANEL), F32),
        pltpu.VMEM((g, RUN, WIDE), F32),
        pltpu.VMEM((g, RUN // 2, WIDE), F32),
        pltpu.VMEM((g, 3, 8, WIDE), F32),
        pltpu.VMEM((g, 8, WIDE), F32),
        pltpu.VMEM((g, 8, WIDE), F32),
        pltpu.VMEM((g, 4, 2, 4, 8, WIDE), F32),
        pltpu.VMEM((g, PIECE, K), F32),
        pltpu.VMEM((n, COLS, K), F32),
        dma((2 + n,)),
    ]
    for shape in (
        (UNITS, 3), (UNITS, 2), (UNITS, 2),
        (n,), (n, 3), (n,),
        (n,), (n, 3), (n,), (n,),
        (g,), (g, 3), (g,), (g, 2), (g, 2), (g, 3), (g,),
        (n, 3), (n,),
    ):
        scratch += [dma(shape), dma(shape)]
    turned = pl.pallas_call(
        kernel,
        out_shape=jax.ShapeDtypeStruct((COLS, ROWS), F32),
        in_specs=[pl.BlockSpec(memory_space=pl.ANY)] * 3,
        out_specs=pl.BlockSpec(memory_space=pl.ANY),
        scratch_shapes=scratch,
        compiler_params=pltpu.CompilerParams(
            collective_id=0, has_side_effects=True, vmem_limit_bytes=58 << 20
        ),
        cost_estimate=pl.CostEstimate(
            flops=2 * 2 * 3 * n * K * ROWS * COLS, bytes_accessed=8 << 20, transcendentals=0
        ),
        name="back_transform",
    )(
        eigvec,
        jnp.transpose(householder, (0, 2, 1)).reshape(n, 2, 8, ROWS),
        panel_factors,
    )
    return turned.T


def solution(mesh):
    in_specs = (P("row", "col"), P(None, "row", "col"), P())
    out_specs = P("row", "col")
    return jax.shard_map(
        per_device, mesh=mesh, in_specs=in_specs, out_specs=out_specs, check_vma=False
    )
```

```python
import functools
import jax
import jax.numpy as jnp
from jax import lax
from jax.experimental import pallas as pl
from jax.experimental.pallas import tpu as pltpu
from jax.sharding import PartitionSpec as P

MESH = pl.DeviceIdType.MESH
F32 = jnp.float32
BF16 = jnp.bfloat16
NT = (((1,), (1,)), ((), ()))
NN = (((1,), (0,)), ((), ()))
BLOCKS = 4
K = 256
PANEL = 128
ROWS = 1792
COLS = 512
HALF = COLS // 2
PIECE = HALF // 4
UNITS = tuple((b, h, 0, ROWS) for b in range(BLOCKS) for h in range(2))
FIRST = {unit[0]: u for u, unit in reversed(list(enumerate(UNITS)))}
LAST = {unit[0]: u for u, unit in enumerate(UNITS)}
RUN = 64
PAIRS = {1: (0,), 2: (1,), 3: (1, 2)}
APPLIED = 0
WIDE = 2 * K
C_HALF = PANEL // 2
ORDER = (
    "z0", "z1", "t0", "y0", "z2", "y1", "z3", "y0", "y2", "z4", "y1", "y3", "z5", "y0", "y2",
    "y4", "z6", "y1", "g1", "c0", "p0", "g1", "p0", "c0", "y3", "y5", "z7", "p0", "g1", "y2",
    "c0", "p0", "y4", "y6", "y3", "g2", "c1", "g1", "c0", "p1", "g2", "c0", "p0", "s0", "p1",
    "c1", "p1", "y4", "g2", "y5", "y7", "s0", "g2", "c1", "y6", "g1", "s0", "y5", "c2", "g3",
    "p1", "c2", "y7", "g2", "c1", "p2", "g3", "p2", "y6", "g1", "p2", "c2", "g3", "y7", "p3",
    "g2", "p3", "g3", "g1", "c2", "p3", "p2", "c3", "g1", "c1", "p1", "s1", "g3", "c3", "g2",
    "g2", "g3", "p3", "c2", "p2", "s2", "s1", "c3", "s1", "g3", "c3", "g3", "c3", "p3", "s3",
    "s2", "s2", "s3", "s3",
)


def split(value):
    high = value.astype(BF16)
    low = (value - high.astype(F32)).astype(BF16)
    return high, low


def dot(a, b, dims):
    return lax.dot_general(a, b, dims, preferred_element_type=F32)


def dot3(a_high, a_low, b_high, b_low, dims):
    small = dot(a_low, b_high, dims) + dot(a_high, b_low, dims)
    return dot(a_high, b_high, dims) + small


def exact(a, b, dims):
    return lax.dot_general(
        a, b, dims, precision=lax.Precision.HIGHEST, preferred_element_type=F32
    )


def kernel(
    z_ref, w_ref, t_ref, out_ref,
    zs, zt, zh, zl, wt, wh, wl, tf,
    pt, rc, rx, ps, rz, cp, cc, cx, cs, cz, cf, gp, gc, gx, gs, gz, gt, fix, st,
    local_sem, zg_s, zg_r, yg_s, yg_r, fg_s, fg_r,
    pc_s, pc_r, px_s, px_r, pz_s, pz_r,
    cc_s, cc_r, cx_s, cx_r, cz_s, cz_r, cf_s, cf_r,
    gc_s, gc_r, gx_s, gx_r, gz_s, gz_r, gy_s, gy_r, gf_s, gf_r, ga_s, ga_r, ge_s, ge_r,
    sx_s, sx_r, sc_s, sc_r,
):
    row, col = lax.axis_index("row"), lax.axis_index("col")
    z_hi, x, core = row // 8, (row // 2) % 4, row % 2
    y, z_lo = col // 4, col % 4

    def at_row(hi, xx, cc_):
        return (hi * 8 + xx * 2 + cc_, col)

    def at_col(yy, zz):
        return (row, yy * 4 + zz)

    sibling = at_row(z_hi, x, 1 - core)
    across = at_row(1 - z_hi, x, core)
    x_peers = [at_row(z_hi, (x + d) % 4, core) for d in (1, 2, 3)]
    z_peers = [at_col(y, (z_lo + d) % 4) for d in (1, 2, 3)]
    y_up, y_down = (y + 1) % 4, (y + 3) % 4
    y_peers = [at_col(y_up, z_lo), at_col(y_down, z_lo)]

    mine = pl.multiple_of(core * HALF, HALF)
    theirs = pl.multiple_of((1 - core) * HALF, HALF)
    piece_rows = pl.ds(pl.multiple_of(mine + x * PIECE, PIECE), PIECE)
    c_mine = pl.ds(pl.multiple_of(core * C_HALF, C_HALF), C_HALF)
    c_theirs = pl.ds(pl.multiple_of((1 - core) * C_HALF, C_HALF), C_HALF)

    sent = []

    def send(src, dst, send_sem, recv_sem, device):
        copy = pltpu.make_async_remote_copy(
            src_ref=src, dst_ref=dst, send_sem=send_sem, recv_sem=recv_sem,
            device_id=device, device_id_type=MESH,
        )
        copy.start()
        sent.append(copy)
        return copy

    def received(copies):
        for copy in copies:
            copy.wait_recv()

    fetch_w = []
    for b in range(BLOCKS):
        copy = pltpu.make_async_copy(w_ref.at[b], wt.at[b, col], local_sem.at[2 + b])
        copy.start()
        fetch_w.append(copy)
    fetch_z = pltpu.make_async_copy(z_ref, zs, local_sem.at[0])
    fetch_z.start()
    fetch_t = pltpu.make_async_copy(t_ref, tf, local_sem.at[1])
    fetch_t.start()

    barrier = pltpu.get_barrier_semaphore()
    peers = [sibling, across] + x_peers + z_peers + y_peers
    for peer in peers:
        pl.semaphore_signal(barrier, inc=1, device_id=peer, device_id_type=MESH)
    pl.semaphore_wait(barrier, len(peers))

    def weights(b):
        @pl.loop(0, ROWS // K)
        def _(i):
            lanes = pl.ds(pl.multiple_of(i * K, K), K)
            both = wt[b, :, :, :, lanes].reshape(K, K)
            wh[b, :, lanes], wl[b, :, lanes] = split(both)

    def project(b, start):
        at = pl.ds(start, HALF)
        pt[b, at, :] = dot3(zh[at, :], zl[at, :], wh[b], wl[b], NT)

    def update(b, start):
        at = pl.ds(start, HALF)
        s_high, s_low = split(st[b, at, :])

        @pl.loop(0, ROWS // K)
        def _(i):
            lanes = pl.ds(pl.multiple_of(i * K, K), K)
            fresh = zt[at, lanes] - dot3(s_high, s_low, wh[b, :, lanes], wl[b, :, lanes], NN)
            zt[at, lanes] = fresh
            if b == APPLIED:
                zh[at, lanes], zl[at, lanes] = split(fresh)

    gathered = [None] * len(UNITS)

    def z_flow(u):
        b, h, at, rows = UNITS[u]
        lanes = pl.ds(at, rows)
        gathered[u] = [
            send(
                w_ref.at[b, h, :, lanes], wt.at[b, col, h, :, lanes],
                zg_s.at[u, d], zg_r.at[u, d], z_peers[d],
            )
            for d in range(3)
        ]
        yield

    def y_flow(u):
        b, h, at, rows = UNITS[u]
        lanes = pl.ds(at, rows)
        if u == FIRST[b]:
            fetch_w[b].wait()
        received(gathered[u])
        run = wt.at[b, pl.ds(4 * y, 4), h, :, lanes]
        up, down = [
            send(run, run, yg_s.at[u, d], yg_r.at[u, d], y_peers[d]) for d in range(2)
        ]
        yield
        up.wait_recv()
        part = wt.at[b, pl.ds(4 * y_down, 2), h, :, lanes]
        one = send(part, part, fg_s.at[u, 0], fg_r.at[u, 0], y_peers[0])
        down.wait_recv()
        part = wt.at[b, pl.ds(4 * y_up + 2, 2), h, :, lanes]
        two = send(part, part, fg_s.at[u, 1], fg_r.at[u, 1], y_peers[1])
        yield
        received([one, two])
        if u == LAST[b]:
            weights(b)
        yield

    def c_flow(b):
        cp[b] = dot3(wh[b, PANEL:, :], wl[b, PANEL:, :], wh[b, :PANEL, :], wl[b, :PANEL, :], NT)
        to_core = send(cp.at[b, c_theirs], cc.at[b], cc_s.at[b], cc_r.at[b], sibling)
        yield
        to_core.wait_recv()
        cp[b, c_mine, :] = cp[b, c_mine, :] + cc[b]
        to_x = [
            send(cp.at[b, c_mine], cx.at[b, d], cx_s.at[b, d], cx_r.at[b, d], x_peers[d])
            for d in range(3)
        ]
        yield
        received(to_x)
        cs[b] = (cp[b, c_mine, :] + cx[b, 0]) + (cx[b, 1] + cx[b, 2])
        to_z = send(cs.at[b], cz.at[b], cz_s.at[b], cz_r.at[b], across)
        yield
        to_z.wait_recv()
        cf[b, c_mine, :] = cs[b] + cz[b]
        part = cf.at[b, c_mine]
        to_core = send(part, part, cf_s.at[b], cf_r.at[b], sibling)
        yield
        to_core.wait_recv()
        yield

    def p_flow(b):
        project(b, theirs)
        to_core = send(
            pt.at[b, pl.ds(theirs, HALF)], rc.at[b], pc_s.at[b], pc_r.at[b], sibling
        )
        yield
        project(b, mine)
        yield
        to_core.wait_recv()
        at = pl.ds(mine, HALF)
        pt[b, at, :] = pt[b, at, :] + rc[b]
        to_x = []
        for d in range(3):
            to = pl.multiple_of(mine + ((x + 1 + d) % 4) * PIECE, PIECE)
            to_x.append(
                send(
                    pt.at[b, pl.ds(to, PIECE)], rx.at[b, d],
                    px_s.at[b, d], px_r.at[b, d], x_peers[d],
                )
            )
        yield
        received(to_x)
        ps[b] = (pt[b, piece_rows, :] + rx[b, 0]) + (rx[b, 1] + rx[b, 2])
        to_z = send(ps.at[b], rz.at[b], pz_s.at[b], pz_r.at[b], across)
        yield
        to_z.wait_recv()
        yield

    def g_flow(b):
        g, wide = b - 1, len(PAIRS[b]) * K
        own = wt[b, pl.ds(4 * y, 4)].reshape(RUN, ROWS)
        own_high, own_low = split(own)
        for i, c in enumerate(PAIRS[b]):
            gp[g, :, i * K : (i + 1) * K] = dot3(own_high, own_low, wh[c], wl[c], NT)
        lanes = pl.ds(0, wide)
        base = pl.multiple_of(core * 32, 32)
        other = pl.multiple_of((1 - core) * 32, 32)
        to_core = send(
            gp.at[g, pl.ds(other, 32), lanes], gc.at[g, :, lanes], gc_s.at[g], gc_r.at[g], sibling
        )
        yield
        to_core.wait_recv()
        at = pl.ds(base, 32)
        gp[g, at, :wide] = gp[g, at, :wide] + gc[g, :, :wide]
        to_x = []
        for d in range(3):
            to = pl.multiple_of(base + ((x + 1 + d) % 4) * 8, 8)
            to_x.append(
                send(
                    gp.at[g, pl.ds(to, 8), lanes], gx.at[g, d, :, lanes],
                    gx_s.at[g, d], gx_r.at[g, d], x_peers[d],
                )
            )
        yield
        received(to_x)
        at = pl.ds(pl.multiple_of(base + x * 8, 8), 8)
        gs[g, :, :wide] = (gp[g, at, :wide] + gx[g, 0, :, :wide]) + (
            gx[g, 1, :, :wide] + gx[g, 2, :, :wide]
        )
        to_z = send(
            gs.at[g, :, lanes], gz.at[g, :, lanes], gz_s.at[g], gz_r.at[g], across
        )
        yield
        to_z.wait_recv()
        gt[g, y, core, x, :, :wide] = gs[g, :, :wide] + gz[g, :, :wide]
        part = gt.at[g, y, core, x, :, lanes]
        up, down = [
            send(part, part, gy_s.at[g, d], gy_r.at[g, d], y_peers[d]) for d in range(2)
        ]
        yield
        up.wait_recv()
        part = gt.at[g, y_down, core, x, :, pl.ds(0, wide // 2)]
        one = send(part, part, gf_s.at[g, 0], gf_r.at[g, 0], y_peers[0])
        down.wait_recv()
        part = gt.at[g, y_up, core, x, :, pl.ds(wide // 2, wide // 2)]
        two = send(part, part, gf_s.at[g, 1], gf_r.at[g, 1], y_peers[1])
        yield
        received([one, two])
        part = gt.at[g, :, core, x, :, lanes]
        to_x = [
            send(part, part, ga_s.at[g, d], ga_r.at[g, d], x_peers[d]) for d in range(3)
        ]
        yield
        received(to_x)
        part = gt.at[g, :, core, :, :, lanes]
        to_core = send(part, part, ge_s.at[g], ge_r.at[g], sibling)
        yield
        to_core.wait_recv()
        total = None
        for i, c in enumerate(PAIRS[b]):
            seen = gt[g, :, :, :, :, i * K : (i + 1) * K].reshape(K, K)
            term = exact(st[c, piece_rows, :], seen, NT)
            total = term if total is None else total + term
        fix[g] = total
        yield

    def s_flow(b):
        total = ps[b] + rz[b]
        if b:
            total = total - fix[b - 1]
        tail = exact(total[:, PANEL:], tf[b, 1], NT)
        lead = exact(total[:, :PANEL] - exact(tail, cf[b], NN), tf[b, 0], NT)
        st[b, piece_rows, :PANEL] = lead
        st[b, piece_rows, PANEL:] = tail
        part = st.at[b, piece_rows]
        to_x = [
            send(part, part, sx_s.at[b, d], sx_r.at[b, d], x_peers[d]) for d in range(3)
        ]
        yield
        received(to_x)
        part = st.at[b, pl.ds(mine, HALF)]
        to_core = send(part, part, sc_s.at[b], sc_r.at[b], sibling)
        if b == BLOCKS - 1:
            update(b, mine)
        yield
        to_core.wait_recv()
        if b < BLOCKS - 1:
            update(b, mine)
        update(b, theirs)
        yield

    def start(_):
        fetch_t.wait()
        fetch_z.wait()

        @pl.loop(0, ROWS // 128)
        def _(i):
            at = pl.ds(pl.multiple_of(i * 128, 128), 128)
            turned = zs[at, :].T
            zt[:, at] = turned
            zh[:, at], zl[:, at] = split(turned)

        yield

    flows = {"t": start, "z": z_flow, "y": y_flow, "c": c_flow, "p": p_flow, "g": g_flow, "s": s_flow}
    steps = {}
    for name in ORDER:
        if name not in steps:
            steps[name] = flows[name[0]](int(name[1:]))
        next(steps[name])

    store = pltpu.make_async_copy(zt, out_ref, local_sem.at[0])
    store.start()
    for copy in sent:
        copy.wait_send()
    store.wait()


def per_device(eigvec, householder, panel_factors):
    dma = pltpu.SemaphoreType.DMA
    n, g = BLOCKS, BLOCKS - 1
    scratch = [
        pltpu.VMEM((ROWS, COLS), F32),
        pltpu.VMEM((COLS, ROWS), F32),
        pltpu.VMEM((COLS, ROWS), BF16),
        pltpu.VMEM((COLS, ROWS), BF16),
        pltpu.VMEM((n, 16, 2, 8, ROWS), F32),
        pltpu.VMEM((n, K, ROWS), BF16),
        pltpu.VMEM((n, K, ROWS), BF16),
        pltpu.VMEM((n, 2, PANEL, PANEL), F32),
        pltpu.VMEM((n, COLS, K), F32),
        pltpu.VMEM((n, HALF, K), F32),
        pltpu.VMEM((n, 3, PIECE, K), F32),
        pltpu.VMEM((n, PIECE, K), F32),
        pltpu.VMEM((n, PIECE, K), F32),
        pltpu.VMEM((n, PANEL, PANEL), F32),
        pltpu.VMEM((n, C_HALF, PANEL), F32),
        pltpu.VMEM((n, 3, C_HALF, PANEL), F32),
        pltpu.VMEM((n, C_HALF, PANEL), F32),
        pltpu.VMEM((n, C_HALF, PANEL), F32),
        pltpu.VMEM((n, PANEL, PANEL), F32),
        pltpu.VMEM((g, RUN, WIDE), F32),
        pltpu.VMEM((g, RUN // 2, WIDE), F32),
        pltpu.VMEM((g, 3, 8, WIDE), F32),
        pltpu.VMEM((g, 8, WIDE), F32),
        pltpu.VMEM((g, 8, WIDE), F32),
        pltpu.VMEM((g, 4, 2, 4, 8, WIDE), F32),
        pltpu.VMEM((g, PIECE, K), F32),
        pltpu.VMEM((n, COLS, K), F32),
        dma((2 + n,)),
    ]
    for shape in (
        (len(UNITS), 3), (len(UNITS), 2), (len(UNITS), 2),
        (n,), (n, 3), (n,),
        (n,), (n, 3), (n,), (n,),
        (g,), (g, 3), (g,), (g, 2), (g, 2), (g, 3), (g,),
        (n, 3), (n,),
    ):
        scratch += [dma(shape), dma(shape)]
    turned = pl.pallas_call(
        kernel,
        out_shape=jax.ShapeDtypeStruct((COLS, ROWS), F32),
        in_specs=[pl.BlockSpec(memory_space=pl.ANY)] * 3,
        out_specs=pl.BlockSpec(memory_space=pl.ANY),
        scratch_shapes=scratch,
        compiler_params=pltpu.CompilerParams(
            collective_id=0, has_side_effects=True, vmem_limit_bytes=58 << 20
        ),
        cost_estimate=pl.CostEstimate(
            flops=2 * 2 * 3 * n * K * ROWS * COLS, bytes_accessed=8 << 20, transcendentals=0
        ),
        name="back_transform",
    )(
        eigvec,
        jnp.transpose(householder, (0, 2, 1)).reshape(n, 2, 8, ROWS),
        panel_factors,
    )
    return turned.T


def solution(mesh):
    in_specs = (P("row", "col"), P(None, "row", "col"), P())
    out_specs = P("row", "col")
    return jax.shard_map(
        per_device, mesh=mesh, in_specs=in_specs, out_specs=out_specs, check_vma=False
    )
```

```python
import functools
import jax
import jax.numpy as jnp
from jax import lax
from jax.experimental import pallas as pl
from jax.experimental.pallas import tpu as pltpu
from jax.sharding import PartitionSpec as P

MESH = pl.DeviceIdType.MESH
F32 = jnp.float32
BF16 = jnp.bfloat16
NT = (((1,), (1,)), ((), ()))
NN = (((1,), (0,)), ((), ()))
BLOCKS = 4
K = 256
PANEL = 128
ROWS = 1792
COLS = 512
HALF = COLS // 2
PIECE = HALF // 4
UNITS = tuple((b, h, 0, ROWS) for b in range(BLOCKS) for h in range(2))
FIRST = {unit[0]: u for u, unit in reversed(list(enumerate(UNITS)))}
LAST = {unit[0]: u for u, unit in enumerate(UNITS)}
RUN = 64
PAIRS = {1: (0,), 2: (1,), 3: (1, 2)}
APPLIED = 0
WIDE = 2 * K
C_HALF = PANEL // 2
ORDER = (
    "z0", "z1", "t0", "y0", "z2", "y1", "z3", "y0", "y2", "z4", "y1", "y3", "z5", "y0", "y2",
    "y4", "z6", "y1", "g1", "c0", "p0", "p0", "c0", "g1", "p0", "y3", "y5", "z7", "y2", "c0",
    "g1", "p0", "y4", "y6", "y3", "g2", "c1", "p1", "c0", "c1", "p1", "g1", "g2", "p1", "y5",
    "y7", "c0", "p0", "s0", "y4", "c1", "g2", "p1", "y6", "g1", "s0", "c1", "g2", "y5", "g3",
    "s0", "g3", "c2", "y7", "p2", "c2", "p2", "g1", "g2", "p2", "g3", "y6", "y7", "c3", "c2",
    "g2", "p3", "c3", "p3", "g1", "p3", "g3", "p2", "g1", "c1", "p1", "s1", "g2", "g3", "c3",
    "c2", "g2", "g3", "p3", "c2", "p2", "s2", "s1", "c3", "g3", "s1", "g3", "c3", "p3", "s3",
    "s2", "s2", "s3", "s3",
)


def split(value):
    high = value.astype(BF16)
    low = (value - high.astype(F32)).astype(BF16)
    return high, low


def dot(a, b, dims):
    return lax.dot_general(a, b, dims, preferred_element_type=F32)


def dot3(a_high, a_low, b_high, b_low, dims):
    small = dot(a_low, b_high, dims) + dot(a_high, b_low, dims)
    return dot(a_high, b_high, dims) + small


def exact(a, b, dims):
    return lax.dot_general(
        a, b, dims, precision=lax.Precision.HIGHEST, preferred_element_type=F32
    )


def kernel(
    z_ref, w_ref, t_ref, out_ref,
    zs, zt, zh, zl, wt, wh, wl, tf,
    pt, rc, rx, ps, rz, cp, cc, cx, cs, cz, cf, gp, gc, gx, gs, gz, gt, fix, st,
    local_sem, zg_s, zg_r, yg_s, yg_r, fg_s, fg_r,
    pc_s, pc_r, px_s, px_r, pz_s, pz_r,
    cc_s, cc_r, cx_s, cx_r, cz_s, cz_r, cf_s, cf_r,
    gc_s, gc_r, gx_s, gx_r, gz_s, gz_r, gy_s, gy_r, gf_s, gf_r, ga_s, ga_r, ge_s, ge_r,
    sx_s, sx_r, sc_s, sc_r,
):
    row, col = lax.axis_index("row"), lax.axis_index("col")
    z_hi, x, core = row // 8, (row // 2) % 4, row % 2
    y, z_lo = col // 4, col % 4

    def at_row(hi, xx, cc_):
        return (hi * 8 + xx * 2 + cc_, col)

    def at_col(yy, zz):
        return (row, yy * 4 + zz)

    sibling = at_row(z_hi, x, 1 - core)
    across = at_row(1 - z_hi, x, core)
    x_peers = [at_row(z_hi, (x + d) % 4, core) for d in (1, 2, 3)]
    z_peers = [at_col(y, (z_lo + d) % 4) for d in (1, 2, 3)]
    y_up, y_down = (y + 1) % 4, (y + 3) % 4
    y_peers = [at_col(y_up, z_lo), at_col(y_down, z_lo)]

    mine = pl.multiple_of(core * HALF, HALF)
    theirs = pl.multiple_of((1 - core) * HALF, HALF)
    piece_rows = pl.ds(pl.multiple_of(mine + x * PIECE, PIECE), PIECE)
    c_mine = pl.ds(pl.multiple_of(core * C_HALF, C_HALF), C_HALF)
    c_theirs = pl.ds(pl.multiple_of((1 - core) * C_HALF, C_HALF), C_HALF)

    sent = []

    def send(src, dst, send_sem, recv_sem, device):
        copy = pltpu.make_async_remote_copy(
            src_ref=src, dst_ref=dst, send_sem=send_sem, recv_sem=recv_sem,
            device_id=device, device_id_type=MESH,
        )
        copy.start()
        sent.append(copy)
        return copy

    def received(copies):
        for copy in copies:
            copy.wait_recv()

    fetch_w = []
    for b in range(BLOCKS):
        copy = pltpu.make_async_copy(w_ref.at[b], wt.at[b, col], local_sem.at[2 + b])
        copy.start()
        fetch_w.append(copy)
    fetch_z = pltpu.make_async_copy(z_ref, zs, local_sem.at[0])
    fetch_z.start()
    fetch_t = pltpu.make_async_copy(t_ref, tf, local_sem.at[1])
    fetch_t.start()

    barrier = pltpu.get_barrier_semaphore()
    peers = [sibling, across] + x_peers + z_peers + y_peers
    for peer in peers:
        pl.semaphore_signal(barrier, inc=1, device_id=peer, device_id_type=MESH)
    pl.semaphore_wait(barrier, len(peers))

    def weights(b):
        @pl.loop(0, ROWS // K)
        def _(i):
            lanes = pl.ds(pl.multiple_of(i * K, K), K)
            both = wt[b, :, :, :, lanes].reshape(K, K)
            wh[b, :, lanes], wl[b, :, lanes] = split(both)

    def project(b, start):
        at = pl.ds(start, HALF)
        pt[b, at, :] = dot3(zh[at, :], zl[at, :], wh[b], wl[b], NT)

    def update(b, start):
        at = pl.ds(start, HALF)
        s_high, s_low = split(st[b, at, :])
        for i in range(ROWS // K):
            lanes = pl.ds(i * K, K)
            fresh = zt[at, lanes] - dot3(s_high, s_low, wh[b, :, lanes], wl[b, :, lanes], NN)
            zt[at, lanes] = fresh
            if b == APPLIED:
                zh[at, lanes], zl[at, lanes] = split(fresh)

    def store(start, sem):
        at = pl.ds(start, HALF)
        copy = pltpu.make_async_copy(zt.at[at], out_ref.at[at], sem)
        copy.start()
        stores.append(copy)

    stores = []
    gathered = [None] * len(UNITS)

    def z_flow(u):
        b, h, at, rows = UNITS[u]
        lanes = pl.ds(at, rows)
        gathered[u] = [
            send(
                w_ref.at[b, h, :, lanes], wt.at[b, col, h, :, lanes],
                zg_s.at[u, d], zg_r.at[u, d], z_peers[d],
            )
            for d in range(3)
        ]
        yield

    def y_flow(u):
        b, h, at, rows = UNITS[u]
        lanes = pl.ds(at, rows)
        if u == FIRST[b]:
            fetch_w[b].wait()
        received(gathered[u])
        run = wt.at[b, pl.ds(4 * y, 4), h, :, lanes]
        up, down = [
            send(run, run, yg_s.at[u, d], yg_r.at[u, d], y_peers[d]) for d in range(2)
        ]
        yield
        up.wait_recv()
        part = wt.at[b, pl.ds(4 * y_down, 2), h, :, lanes]
        one = send(part, part, fg_s.at[u, 0], fg_r.at[u, 0], y_peers[0])
        down.wait_recv()
        part = wt.at[b, pl.ds(4 * y_up + 2, 2), h, :, lanes]
        two = send(part, part, fg_s.at[u, 1], fg_r.at[u, 1], y_peers[1])
        yield
        received([one, two])
        if u == LAST[b]:
            weights(b)
        yield

    def c_flow(b):
        cp[b] = dot3(wh[b, PANEL:, :], wl[b, PANEL:, :], wh[b, :PANEL, :], wl[b, :PANEL, :], NT)
        to_core = send(cp.at[b, c_theirs], cc.at[b], cc_s.at[b], cc_r.at[b], sibling)
        yield
        to_core.wait_recv()
        cp[b, c_mine, :] = cp[b, c_mine, :] + cc[b]
        to_x = [
            send(cp.at[b, c_mine], cx.at[b, d], cx_s.at[b, d], cx_r.at[b, d], x_peers[d])
            for d in range(3)
        ]
        yield
        received(to_x)
        cs[b] = (cp[b, c_mine, :] + cx[b, 0]) + (cx[b, 1] + cx[b, 2])
        to_z = send(cs.at[b], cz.at[b], cz_s.at[b], cz_r.at[b], across)
        yield
        to_z.wait_recv()
        cf[b, c_mine, :] = cs[b] + cz[b]
        part = cf.at[b, c_mine]
        to_core = send(part, part, cf_s.at[b], cf_r.at[b], sibling)
        yield
        to_core.wait_recv()
        yield

    def p_flow(b):
        project(b, theirs)
        to_core = send(
            pt.at[b, pl.ds(theirs, HALF)], rc.at[b], pc_s.at[b], pc_r.at[b], sibling
        )
        yield
        project(b, mine)
        yield
        to_core.wait_recv()
        at = pl.ds(mine, HALF)
        pt[b, at, :] = pt[b, at, :] + rc[b]
        to_x = []
        for d in range(3):
            to = pl.multiple_of(mine + ((x + 1 + d) % 4) * PIECE, PIECE)
            to_x.append(
                send(
                    pt.at[b, pl.ds(to, PIECE)], rx.at[b, d],
                    px_s.at[b, d], px_r.at[b, d], x_peers[d],
                )
            )
        yield
        received(to_x)
        ps[b] = (pt[b, piece_rows, :] + rx[b, 0]) + (rx[b, 1] + rx[b, 2])
        to_z = send(ps.at[b], rz.at[b], pz_s.at[b], pz_r.at[b], across)
        yield
        to_z.wait_recv()
        yield

    def g_flow(b):
        g, wide = b - 1, len(PAIRS[b]) * K
        own = wt[b, pl.ds(4 * y, 4)].reshape(RUN, ROWS)
        own_high, own_low = split(own)
        for i, c in enumerate(PAIRS[b]):
            gp[g, :, i * K : (i + 1) * K] = dot3(own_high, own_low, wh[c], wl[c], NT)
        lanes = pl.ds(0, wide)
        base = pl.multiple_of(core * 32, 32)
        other = pl.multiple_of((1 - core) * 32, 32)
        to_core = send(
            gp.at[g, pl.ds(other, 32), lanes], gc.at[g, :, lanes], gc_s.at[g], gc_r.at[g], sibling
        )
        yield
        to_core.wait_recv()
        at = pl.ds(base, 32)
        gp[g, at, :wide] = gp[g, at, :wide] + gc[g, :, :wide]
        to_x = []
        for d in range(3):
            to = pl.multiple_of(base + ((x + 1 + d) % 4) * 8, 8)
            to_x.append(
                send(
                    gp.at[g, pl.ds(to, 8), lanes], gx.at[g, d, :, lanes],
                    gx_s.at[g, d], gx_r.at[g, d], x_peers[d],
                )
            )
        yield
        received(to_x)
        at = pl.ds(pl.multiple_of(base + x * 8, 8), 8)
        gs[g, :, :wide] = (gp[g, at, :wide] + gx[g, 0, :, :wide]) + (
            gx[g, 1, :, :wide] + gx[g, 2, :, :wide]
        )
        to_z = send(
            gs.at[g, :, lanes], gz.at[g, :, lanes], gz_s.at[g], gz_r.at[g], across
        )
        yield
        to_z.wait_recv()
        gt[g, y, core, x, :, :wide] = gs[g, :, :wide] + gz[g, :, :wide]
        part = gt.at[g, y, core, x, :, lanes]
        up, down = [
            send(part, part, gy_s.at[g, d], gy_r.at[g, d], y_peers[d]) for d in range(2)
        ]
        yield
        up.wait_recv()
        part = gt.at[g, y_down, core, x, :, pl.ds(0, wide // 2)]
        one = send(part, part, gf_s.at[g, 0], gf_r.at[g, 0], y_peers[0])
        down.wait_recv()
        part = gt.at[g, y_up, core, x, :, pl.ds(wide // 2, wide // 2)]
        two = send(part, part, gf_s.at[g, 1], gf_r.at[g, 1], y_peers[1])
        yield
        received([one, two])
        part = gt.at[g, :, core, x, :, lanes]
        to_x = [
            send(part, part, ga_s.at[g, d], ga_r.at[g, d], x_peers[d]) for d in range(3)
        ]
        yield
        received(to_x)
        part = gt.at[g, :, core, :, :, lanes]
        to_core = send(part, part, ge_s.at[g], ge_r.at[g], sibling)
        yield
        to_core.wait_recv()
        total = None
        for i, c in enumerate(PAIRS[b]):
            seen = gt[g, :, :, :, :, i * K : (i + 1) * K].reshape(K, K)
            term = exact(st[c, piece_rows, :], seen, NT)
            total = term if total is None else total + term
        fix[g] = total
        yield

    def s_flow(b):
        total = ps[b] + rz[b]
        if b:
            total = total - fix[b - 1]
        tail = exact(total[:, PANEL:], tf[b, 1], NT)
        lead = exact(total[:, :PANEL] - exact(tail, cf[b], NN), tf[b, 0], NT)
        st[b, piece_rows, :PANEL] = lead
        st[b, piece_rows, PANEL:] = tail
        part = st.at[b, piece_rows]
        to_x = [
            send(part, part, sx_s.at[b, d], sx_r.at[b, d], x_peers[d]) for d in range(3)
        ]
        yield
        received(to_x)
        part = st.at[b, pl.ds(mine, HALF)]
        to_core = send(part, part, sc_s.at[b], sc_r.at[b], sibling)
        if b == BLOCKS - 1:
            update(b, mine)
            store(mine, local_sem.at[0])
        yield
        to_core.wait_recv()
        if b < BLOCKS - 1:
            update(b, mine)
        update(b, theirs)
        if b == BLOCKS - 1:
            store(theirs, local_sem.at[1])
        yield

    def start(_):
        fetch_t.wait()
        fetch_z.wait()

        @pl.loop(0, ROWS // 128)
        def _(i):
            at = pl.ds(pl.multiple_of(i * 128, 128), 128)
            turned = zs[at, :].T
            zt[:, at] = turned
            zh[:, at], zl[:, at] = split(turned)

        yield

    flows = {"t": start, "z": z_flow, "y": y_flow, "c": c_flow, "p": p_flow, "g": g_flow, "s": s_flow}
    steps = {}
    for name in ORDER:
        if name not in steps:
            steps[name] = flows[name[0]](int(name[1:]))
        next(steps[name])

    for copy in sent:
        copy.wait_send()
    for copy in stores:
        copy.wait()


def per_device(eigvec, householder, panel_factors):
    dma = pltpu.SemaphoreType.DMA
    n, g = BLOCKS, BLOCKS - 1
    scratch = [
        pltpu.VMEM((ROWS, COLS), F32),
        pltpu.VMEM((COLS, ROWS), F32),
        pltpu.VMEM((COLS, ROWS), BF16),
        pltpu.VMEM((COLS, ROWS), BF16),
        pltpu.VMEM((n, 16, 2, 8, ROWS), F32),
        pltpu.VMEM((n, K, ROWS), BF16),
        pltpu.VMEM((n, K, ROWS), BF16),
        pltpu.VMEM((n, 2, PANEL, PANEL), F32),
        pltpu.VMEM((n, COLS, K), F32),
        pltpu.VMEM((n, HALF, K), F32),
        pltpu.VMEM((n, 3, PIECE, K), F32),
        pltpu.VMEM((n, PIECE, K), F32),
        pltpu.VMEM((n, PIECE, K), F32),
        pltpu.VMEM((n, PANEL, PANEL), F32),
        pltpu.VMEM((n, C_HALF, PANEL), F32),
        pltpu.VMEM((n, 3, C_HALF, PANEL), F32),
        pltpu.VMEM((n, C_HALF, PANEL), F32),
        pltpu.VMEM((n, C_HALF, PANEL), F32),
        pltpu.VMEM((n, PANEL, PANEL), F32),
        pltpu.VMEM((g, RUN, WIDE), F32),
        pltpu.VMEM((g, RUN // 2, WIDE), F32),
        pltpu.VMEM((g, 3, 8, WIDE), F32),
        pltpu.VMEM((g, 8, WIDE), F32),
        pltpu.VMEM((g, 8, WIDE), F32),
        pltpu.VMEM((g, 4, 2, 4, 8, WIDE), F32),
        pltpu.VMEM((g, PIECE, K), F32),
        pltpu.VMEM((n, COLS, K), F32),
        dma((2 + n,)),
    ]
    for shape in (
        (len(UNITS), 3), (len(UNITS), 2), (len(UNITS), 2),
        (n,), (n, 3), (n,),
        (n,), (n, 3), (n,), (n,),
        (g,), (g, 3), (g,), (g, 2), (g, 2), (g, 3), (g,),
        (n, 3), (n,),
    ):
        scratch += [dma(shape), dma(shape)]
    turned = pl.pallas_call(
        kernel,
        out_shape=jax.ShapeDtypeStruct((COLS, ROWS), F32),
        in_specs=[pl.BlockSpec(memory_space=pl.ANY)] * 3,
        out_specs=pl.BlockSpec(memory_space=pl.ANY),
        scratch_shapes=scratch,
        compiler_params=pltpu.CompilerParams(
            collective_id=0, has_side_effects=True, vmem_limit_bytes=58 << 20
        ),
        cost_estimate=pl.CostEstimate(
            flops=2 * 2 * 3 * n * K * ROWS * COLS, bytes_accessed=8 << 20, transcendentals=0
        ),
        name="back_transform",
    )(
        eigvec,
        jnp.transpose(householder, (0, 2, 1)).reshape(n, 2, 8, ROWS),
        panel_factors,
    )
    return turned.T


def solution(mesh):
    in_specs = (P("row", "col"), P(None, "row", "col"), P())
    out_specs = P("row", "col")
    return jax.shard_map(
        per_device, mesh=mesh, in_specs=in_specs, out_specs=out_specs, check_vma=False
    )
```

```python
import functools
import jax
import jax.numpy as jnp
from jax import lax
from jax.experimental import pallas as pl
from jax.experimental.pallas import tpu as pltpu
from jax.sharding import PartitionSpec as P

MESH = pl.DeviceIdType.MESH
F32 = jnp.float32
BF16 = jnp.bfloat16
NT = (((1,), (1,)), ((), ()))
NN = (((1,), (0,)), ((), ()))
BLOCKS = 4
K = 256
PANEL = 128
ROWS = 1792
COLS = 512
HALF = COLS // 2
PIECE = HALF // 4
UNITS = tuple((b, h, 0, ROWS) for b in range(BLOCKS) for h in range(2))
FIRST = {unit[0]: u for u, unit in reversed(list(enumerate(UNITS)))}
LAST = {unit[0]: u for u, unit in enumerate(UNITS)}
RUN = 64
PAIRS = {1: (0,), 2: (1,), 3: (1, 2)}
APPLIED = 0
WIDE = 2 * K
C_HALF = PANEL // 2
ORDER = (
    "z0", "z1", "t0", "y0", "z2", "y1", "z3", "y0", "y2", "z4", "y1", "y3", "z5", "y0", "y2",
    "y4", "z6", "y1", "g1", "c0", "p0", "p0", "c0", "g1", "p0", "y3", "y5", "z7", "y2", "c0",
    "g1", "p0", "y4", "y6", "y3", "g2", "c1", "p1", "c0", "c1", "p1", "g1", "g2", "p1", "y5",
    "y7", "c0", "p0", "s0", "y4", "c1", "g2", "p1", "y6", "g1", "s0", "c1", "g2", "y5", "g3",
    "s0", "g3", "c2", "y7", "p2", "c2", "p2", "g1", "g2", "p2", "g3", "y6", "y7", "c3", "c2",
    "g2", "p3", "c3", "p3", "g1", "p3", "g3", "p2", "g1", "c1", "p1", "s1", "g2", "g3", "c3",
    "c2", "g2", "g3", "p3", "c2", "p2", "s2", "s1", "c3", "g3", "g3", "c3", "p3", "s3", "s2",
    "s1", "s2", "s3", "s3",
)


def split(value):
    high = value.astype(BF16)
    low = (value - high.astype(F32)).astype(BF16)
    return high, low


def dot(a, b, dims):
    return lax.dot_general(a, b, dims, preferred_element_type=F32)


def dot3(a_high, a_low, b_high, b_low, dims):
    small = dot(a_low, b_high, dims) + dot(a_high, b_low, dims)
    return dot(a_high, b_high, dims) + small


def exact(a, b, dims):
    return lax.dot_general(
        a, b, dims, precision=lax.Precision.HIGHEST, preferred_element_type=F32
    )


def kernel(
    z_ref, w_ref, t_ref, out_ref,
    zs, zt, zh, zl, wt, wh, wl, tf,
    pt, rc, rx, ps, rz, cp, cc, cx, cs, cz, cf, gp, gc, gx, gs, gz, gt, fix, st,
    local_sem, zg_s, zg_r, yg_s, yg_r, fg_s, fg_r,
    pc_s, pc_r, px_s, px_r, pz_s, pz_r,
    cc_s, cc_r, cx_s, cx_r, cz_s, cz_r, cf_s, cf_r,
    gc_s, gc_r, gx_s, gx_r, gz_s, gz_r, gy_s, gy_r, gf_s, gf_r, ga_s, ga_r, ge_s, ge_r,
    sx_s, sx_r, sc_s, sc_r,
):
    row, col = lax.axis_index("row"), lax.axis_index("col")
    z_hi, x, core = row // 8, (row // 2) % 4, row % 2
    y, z_lo = col // 4, col % 4

    def at_row(hi, xx, cc_):
        return (hi * 8 + xx * 2 + cc_, col)

    def at_col(yy, zz):
        return (row, yy * 4 + zz)

    sibling = at_row(z_hi, x, 1 - core)
    across = at_row(1 - z_hi, x, core)
    x_peers = [at_row(z_hi, (x + d) % 4, core) for d in (1, 2, 3)]
    z_peers = [at_col(y, (z_lo + d) % 4) for d in (1, 2, 3)]
    y_up, y_down = (y + 1) % 4, (y + 3) % 4
    y_peers = [at_col(y_up, z_lo), at_col(y_down, z_lo)]

    mine = pl.multiple_of(core * HALF, HALF)
    theirs = pl.multiple_of((1 - core) * HALF, HALF)
    piece_rows = pl.ds(pl.multiple_of(mine + x * PIECE, PIECE), PIECE)
    c_mine = pl.ds(pl.multiple_of(core * C_HALF, C_HALF), C_HALF)
    c_theirs = pl.ds(pl.multiple_of((1 - core) * C_HALF, C_HALF), C_HALF)

    sent = []

    def send(src, dst, send_sem, recv_sem, device):
        copy = pltpu.make_async_remote_copy(
            src_ref=src, dst_ref=dst, send_sem=send_sem, recv_sem=recv_sem,
            device_id=device, device_id_type=MESH,
        )
        copy.start()
        sent.append(copy)
        return copy

    def received(copies):
        for copy in copies:
            copy.wait_recv()

    fetch_w = []
    for b in range(BLOCKS):
        copy = pltpu.make_async_copy(w_ref.at[b], wt.at[b, col], local_sem.at[2 + b])
        copy.start()
        fetch_w.append(copy)
    fetch_z = pltpu.make_async_copy(z_ref, zs, local_sem.at[0])
    fetch_z.start()
    fetch_t = pltpu.make_async_copy(t_ref, tf, local_sem.at[1])
    fetch_t.start()

    barrier = pltpu.get_barrier_semaphore()
    peers = [sibling, across] + x_peers + z_peers + y_peers
    for peer in peers:
        pl.semaphore_signal(barrier, inc=1, device_id=peer, device_id_type=MESH)
    pl.semaphore_wait(barrier, len(peers))

    def weights(b):
        @pl.loop(0, ROWS // K)
        def _(i):
            lanes = pl.ds(pl.multiple_of(i * K, K), K)
            both = wt[b, :, :, :, lanes].reshape(K, K)
            wh[b, :, lanes], wl[b, :, lanes] = split(both)

    def project(b, start):
        at = pl.ds(start, HALF)
        pt[b, at, :] = dot3(zh[at, :], zl[at, :], wh[b], wl[b], NT)

    def update(b, start):
        at = pl.ds(start, HALF)
        s_high, s_low = split(st[b, at, :])
        for i in range(ROWS // K):
            lanes = pl.ds(i * K, K)
            fresh = zt[at, lanes] - dot3(s_high, s_low, wh[b, :, lanes], wl[b, :, lanes], NN)
            zt[at, lanes] = fresh
            if b == APPLIED:
                zh[at, lanes], zl[at, lanes] = split(fresh)

    def store(start, sem):
        at = pl.ds(start, HALF)
        copy = pltpu.make_async_copy(zt.at[at], out_ref.at[at], sem)
        copy.start()
        stores.append(copy)

    stores = []
    gathered = [None] * len(UNITS)

    def z_flow(u):
        b, h, at, rows = UNITS[u]
        lanes = pl.ds(at, rows)
        gathered[u] = [
            send(
                w_ref.at[b, h, :, lanes], wt.at[b, col, h, :, lanes],
                zg_s.at[u, d], zg_r.at[u, d], z_peers[d],
            )
            for d in range(3)
        ]
        yield

    def y_flow(u):
        b, h, at, rows = UNITS[u]
        lanes = pl.ds(at, rows)
        if u == FIRST[b]:
            fetch_w[b].wait()
        received(gathered[u])
        run = wt.at[b, pl.ds(4 * y, 4), h, :, lanes]
        up, down = [
            send(run, run, yg_s.at[u, d], yg_r.at[u, d], y_peers[d]) for d in range(2)
        ]
        yield
        up.wait_recv()
        part = wt.at[b, pl.ds(4 * y_down, 2), h, :, lanes]
        one = send(part, part, fg_s.at[u, 0], fg_r.at[u, 0], y_peers[0])
        down.wait_recv()
        part = wt.at[b, pl.ds(4 * y_up + 2, 2), h, :, lanes]
        two = send(part, part, fg_s.at[u, 1], fg_r.at[u, 1], y_peers[1])
        yield
        received([one, two])
        if u == LAST[b]:
            weights(b)
        yield

    def c_flow(b):
        cp[b] = dot3(wh[b, PANEL:, :], wl[b, PANEL:, :], wh[b, :PANEL, :], wl[b, :PANEL, :], NT)
        to_core = send(cp.at[b, c_theirs], cc.at[b], cc_s.at[b], cc_r.at[b], sibling)
        yield
        to_core.wait_recv()
        cp[b, c_mine, :] = cp[b, c_mine, :] + cc[b]
        to_x = [
            send(cp.at[b, c_mine], cx.at[b, d], cx_s.at[b, d], cx_r.at[b, d], x_peers[d])
            for d in range(3)
        ]
        yield
        received(to_x)
        cs[b] = (cp[b, c_mine, :] + cx[b, 0]) + (cx[b, 1] + cx[b, 2])
        to_z = send(cs.at[b], cz.at[b], cz_s.at[b], cz_r.at[b], across)
        yield
        to_z.wait_recv()
        cf[b, c_mine, :] = cs[b] + cz[b]
        part = cf.at[b, c_mine]
        to_core = send(part, part, cf_s.at[b], cf_r.at[b], sibling)
        yield
        to_core.wait_recv()
        yield

    def p_flow(b):
        project(b, theirs)
        to_core = send(
            pt.at[b, pl.ds(theirs, HALF)], rc.at[b], pc_s.at[b], pc_r.at[b], sibling
        )
        yield
        project(b, mine)
        yield
        to_core.wait_recv()
        at = pl.ds(mine, HALF)
        pt[b, at, :] = pt[b, at, :] + rc[b]
        to_x = []
        for d in range(3):
            to = pl.multiple_of(mine + ((x + 1 + d) % 4) * PIECE, PIECE)
            to_x.append(
                send(
                    pt.at[b, pl.ds(to, PIECE)], rx.at[b, d],
                    px_s.at[b, d], px_r.at[b, d], x_peers[d],
                )
            )
        yield
        received(to_x)
        ps[b] = (pt[b, piece_rows, :] + rx[b, 0]) + (rx[b, 1] + rx[b, 2])
        to_z = send(ps.at[b], rz.at[b], pz_s.at[b], pz_r.at[b], across)
        yield
        to_z.wait_recv()
        yield

    def g_flow(b):
        g, wide = b - 1, len(PAIRS[b]) * K
        own = wt[b, pl.ds(4 * y, 4)].reshape(RUN, ROWS)
        own_high, own_low = split(own)
        for i, c in enumerate(PAIRS[b]):
            gp[g, :, i * K : (i + 1) * K] = dot3(own_high, own_low, wh[c], wl[c], NT)
        lanes = pl.ds(0, wide)
        base = pl.multiple_of(core * 32, 32)
        other = pl.multiple_of((1 - core) * 32, 32)
        to_core = send(
            gp.at[g, pl.ds(other, 32), lanes], gc.at[g, :, lanes], gc_s.at[g], gc_r.at[g], sibling
        )
        yield
        to_core.wait_recv()
        at = pl.ds(base, 32)
        gp[g, at, :wide] = gp[g, at, :wide] + gc[g, :, :wide]
        to_x = []
        for d in range(3):
            to = pl.multiple_of(base + ((x + 1 + d) % 4) * 8, 8)
            to_x.append(
                send(
                    gp.at[g, pl.ds(to, 8), lanes], gx.at[g, d, :, lanes],
                    gx_s.at[g, d], gx_r.at[g, d], x_peers[d],
                )
            )
        yield
        received(to_x)
        at = pl.ds(pl.multiple_of(base + x * 8, 8), 8)
        gs[g, :, :wide] = (gp[g, at, :wide] + gx[g, 0, :, :wide]) + (
            gx[g, 1, :, :wide] + gx[g, 2, :, :wide]
        )
        to_z = send(
            gs.at[g, :, lanes], gz.at[g, :, lanes], gz_s.at[g], gz_r.at[g], across
        )
        yield
        to_z.wait_recv()
        gt[g, y, core, x, :, :wide] = gs[g, :, :wide] + gz[g, :, :wide]
        part = gt.at[g, y, core, x, :, lanes]
        up, down = [
            send(part, part, gy_s.at[g, d], gy_r.at[g, d], y_peers[d]) for d in range(2)
        ]
        yield
        up.wait_recv()
        part = gt.at[g, y_down, core, x, :, pl.ds(0, wide // 2)]
        one = send(part, part, gf_s.at[g, 0], gf_r.at[g, 0], y_peers[0])
        down.wait_recv()
        part = gt.at[g, y_up, core, x, :, pl.ds(wide // 2, wide // 2)]
        two = send(part, part, gf_s.at[g, 1], gf_r.at[g, 1], y_peers[1])
        yield
        received([one, two])
        part = gt.at[g, :, core, x, :, lanes]
        to_x = [
            send(part, part, ga_s.at[g, d], ga_r.at[g, d], x_peers[d]) for d in range(3)
        ]
        yield
        received(to_x)
        part = gt.at[g, :, core, :, :, lanes]
        to_core = send(part, part, ge_s.at[g], ge_r.at[g], sibling)
        yield
        to_core.wait_recv()
        total = None
        for i, c in enumerate(PAIRS[b]):
            seen = gt[g, :, :, :, :, i * K : (i + 1) * K].reshape(K, K)
            term = exact(st[c, piece_rows, :], seen, NT)
            total = term if total is None else total + term
        fix[g] = total
        yield

    def s_flow(b):
        total = ps[b] + rz[b]
        if b:
            total = total - fix[b - 1]
        tail = exact(total[:, PANEL:], tf[b, 1], NT)
        lead = exact(total[:, :PANEL] - exact(tail, cf[b], NN), tf[b, 0], NT)
        st[b, piece_rows, :PANEL] = lead
        st[b, piece_rows, PANEL:] = tail
        part = st.at[b, piece_rows]
        to_x = [
            send(part, part, sx_s.at[b, d], sx_r.at[b, d], x_peers[d]) for d in range(3)
        ]
        yield
        received(to_x)
        part = st.at[b, pl.ds(mine, HALF)]
        to_core = send(part, part, sc_s.at[b], sc_r.at[b], sibling)
        if b == BLOCKS - 1:
            update(b, mine)
            store(mine, local_sem.at[0])
        yield
        to_core.wait_recv()
        if b < BLOCKS - 1:
            update(b, mine)
        update(b, theirs)
        if b == BLOCKS - 1:
            store(theirs, local_sem.at[1])
        yield

    def start(_):
        fetch_t.wait()
        fetch_z.wait()

        @pl.loop(0, ROWS // 128)
        def _(i):
            at = pl.ds(pl.multiple_of(i * 128, 128), 128)
            turned = zs[at, :].T
            zt[:, at] = turned
            zh[:, at], zl[:, at] = split(turned)

        yield

    flows = {"t": start, "z": z_flow, "y": y_flow, "c": c_flow, "p": p_flow, "g": g_flow, "s": s_flow}
    steps = {}
    for name in ORDER:
        if name not in steps:
            steps[name] = flows[name[0]](int(name[1:]))
        next(steps[name])

    for copy in sent:
        copy.wait_send()
    for copy in stores:
        copy.wait()


def per_device(eigvec, householder, panel_factors):
    dma = pltpu.SemaphoreType.DMA
    n, g = BLOCKS, BLOCKS - 1
    scratch = [
        pltpu.VMEM((ROWS, COLS), F32),
        pltpu.VMEM((COLS, ROWS), F32),
        pltpu.VMEM((COLS, ROWS), BF16),
        pltpu.VMEM((COLS, ROWS), BF16),
        pltpu.VMEM((n, 16, 2, 8, ROWS), F32),
        pltpu.VMEM((n, K, ROWS), BF16),
        pltpu.VMEM((n, K, ROWS), BF16),
        pltpu.VMEM((n, 2, PANEL, PANEL), F32),
        pltpu.VMEM((n, COLS, K), F32),
        pltpu.VMEM((n, HALF, K), F32),
        pltpu.VMEM((n, 3, PIECE, K), F32),
        pltpu.VMEM((n, PIECE, K), F32),
        pltpu.VMEM((n, PIECE, K), F32),
        pltpu.VMEM((n, PANEL, PANEL), F32),
        pltpu.VMEM((n, C_HALF, PANEL), F32),
        pltpu.VMEM((n, 3, C_HALF, PANEL), F32),
        pltpu.VMEM((n, C_HALF, PANEL), F32),
        pltpu.VMEM((n, C_HALF, PANEL), F32),
        pltpu.VMEM((n, PANEL, PANEL), F32),
        pltpu.VMEM((g, RUN, WIDE), F32),
        pltpu.VMEM((g, RUN // 2, WIDE), F32),
        pltpu.VMEM((g, 3, 8, WIDE), F32),
        pltpu.VMEM((g, 8, WIDE), F32),
        pltpu.VMEM((g, 8, WIDE), F32),
        pltpu.VMEM((g, 4, 2, 4, 8, WIDE), F32),
        pltpu.VMEM((g, PIECE, K), F32),
        pltpu.VMEM((n, COLS, K), F32),
        dma((2 + n,)),
    ]
    for shape in (
        (len(UNITS), 3), (len(UNITS), 2), (len(UNITS), 2),
        (n,), (n, 3), (n,),
        (n,), (n, 3), (n,), (n,),
        (g,), (g, 3), (g,), (g, 2), (g, 2), (g, 3), (g,),
        (n, 3), (n,),
    ):
        scratch += [dma(shape), dma(shape)]
    turned = pl.pallas_call(
        kernel,
        out_shape=jax.ShapeDtypeStruct((COLS, ROWS), F32),
        in_specs=[pl.BlockSpec(memory_space=pl.ANY)] * 3,
        out_specs=pl.BlockSpec(memory_space=pl.ANY),
        scratch_shapes=scratch,
        compiler_params=pltpu.CompilerParams(
            collective_id=0, has_side_effects=True, vmem_limit_bytes=58 << 20
        ),
        cost_estimate=pl.CostEstimate(
            flops=2 * 2 * 3 * n * K * ROWS * COLS, bytes_accessed=8 << 20, transcendentals=0
        ),
        name="back_transform",
    )(
        eigvec,
        jnp.transpose(householder, (0, 2, 1)).reshape(n, 2, 8, ROWS),
        panel_factors,
    )
    return turned.T


def solution(mesh):
    in_specs = (P("row", "col"), P(None, "row", "col"), P())
    out_specs = P("row", "col")
    return jax.shard_map(
        per_device, mesh=mesh, in_specs=in_specs, out_specs=out_specs, check_vma=False
    )
```

```python
import functools
import jax
import jax.numpy as jnp
from jax import lax
from jax.experimental import pallas as pl
from jax.experimental.pallas import tpu as pltpu
from jax.sharding import PartitionSpec as P

MESH = pl.DeviceIdType.MESH
F32 = jnp.float32
BF16 = jnp.bfloat16
NT = (((1,), (1,)), ((), ()))
NN = (((1,), (0,)), ((), ()))
BLOCKS = 4
K = 256
PANEL = 128
ROWS = 1792
COLS = 512
HALF = COLS // 2
PIECE = HALF // 4
UNITS = tuple((b, h, 0, ROWS) for b in range(BLOCKS) for h in range(2))
FIRST = {unit[0]: u for u, unit in reversed(list(enumerate(UNITS)))}
LAST = {unit[0]: u for u, unit in enumerate(UNITS)}
RUN = 64
PAIRS = {1: (0,), 2: (1,), 3: (1, 2)}
APPLIED = 0
WIDE = 2 * K
C_HALF = PANEL // 2
ORDER = (
    "z0", "z1", "t0", "y0", "z2", "y1", "z3", "y0", "y2", "z4", "y1", "y3", "z5", "y0", "y2",
    "y4", "z6", "y1", "g1", "c0", "p0", "p0", "c0", "g1", "p0", "y3", "y5", "z7", "y2", "c0",
    "g1", "p0", "y4", "y6", "y3", "g2", "c1", "p1", "c0", "c1", "p1", "g1", "g2", "p1", "y5",
    "y7", "c0", "p0", "s0", "y4", "c1", "g2", "p1", "y6", "g1", "s0", "c1", "g2", "y5", "g3",
    "s0", "g3", "c2", "y7", "p2", "c2", "p2", "g1", "g2", "p2", "g3", "y6", "y7", "c3", "c2",
    "g2", "p3", "c3", "p3", "g1", "p3", "g3", "p2", "g1", "c1", "p1", "s1", "g2", "g3", "c3",
    "c2", "g2", "g3", "p3", "c2", "p2", "s2", "s1", "c3", "g3", "g3", "c3", "p3", "s3", "s2",
    "s1", "s2", "s3", "s3",
)


def split(value):
    high = value.astype(BF16)
    low = (value - high.astype(F32)).astype(BF16)
    return high, low


def dot(a, b, dims):
    return lax.dot_general(a, b, dims, preferred_element_type=F32)


def dot3(a_high, a_low, b_high, b_low, dims):
    small = dot(a_low, b_high, dims) + dot(a_high, b_low, dims)
    return dot(a_high, b_high, dims) + small


def exact(a, b, dims):
    return lax.dot_general(
        a, b, dims, precision=lax.Precision.HIGHEST, preferred_element_type=F32
    )


def kernel(
    z_ref, w_ref, t_ref, out_ref,
    zs, zt, zh, zl, wt, wh, wl, tf,
    pt, rc, rx, ps, rz, cp, cc, cx, cs, cz, cf, gp, gc, gx, gs, gz, gt, fix, st,
    local_sem, zg_s, zg_r, yg_s, yg_r, fg_s, fg_r,
    pc_s, pc_r, px_s, px_r, pz_s, pz_r,
    cc_s, cc_r, cx_s, cx_r, cz_s, cz_r, cf_s, cf_r,
    gc_s, gc_r, gx_s, gx_r, gz_s, gz_r, gy_s, gy_r, gf_s, gf_r, ga_s, ga_r, ge_s, ge_r,
    sx_s, sx_r, sc_s, sc_r,
):
    row, col = lax.axis_index("row"), lax.axis_index("col")
    z_hi, x, core = row // 8, (row // 2) % 4, row % 2
    y, z_lo = col // 4, col % 4

    def at_row(hi, xx, cc_):
        return (hi * 8 + xx * 2 + cc_, col)

    def at_col(yy, zz):
        return (row, yy * 4 + zz)

    sibling = at_row(z_hi, x, 1 - core)
    across = at_row(1 - z_hi, x, core)
    x_peers = [at_row(z_hi, (x + d) % 4, core) for d in (1, 2, 3)]
    z_peers = [at_col(y, (z_lo + d) % 4) for d in (1, 2, 3)]
    y_up, y_down = (y + 1) % 4, (y + 3) % 4
    y_peers = [at_col(y_up, z_lo), at_col(y_down, z_lo)]

    mine = pl.multiple_of(core * HALF, HALF)
    theirs = pl.multiple_of((1 - core) * HALF, HALF)
    piece_rows = pl.ds(pl.multiple_of(mine + x * PIECE, PIECE), PIECE)
    c_mine = pl.ds(pl.multiple_of(core * C_HALF, C_HALF), C_HALF)
    c_theirs = pl.ds(pl.multiple_of((1 - core) * C_HALF, C_HALF), C_HALF)

    sent = []

    def send(src, dst, send_sem, recv_sem, device):
        copy = pltpu.make_async_remote_copy(
            src_ref=src, dst_ref=dst, send_sem=send_sem, recv_sem=recv_sem,
            device_id=device, device_id_type=MESH,
        )
        copy.start()
        sent.append(copy)
        return copy

    def received(copies):
        for copy in copies:
            copy.wait_recv()

    fetch_w = []
    for b in range(BLOCKS):
        copy = pltpu.make_async_copy(w_ref.at[b], wt.at[b, col], local_sem.at[2 + b])
        copy.start()
        fetch_w.append(copy)
    fetch_z = pltpu.make_async_copy(z_ref, zs, local_sem.at[0])
    fetch_z.start()
    fetch_t = pltpu.make_async_copy(t_ref, tf, local_sem.at[1])
    fetch_t.start()

    barrier = pltpu.get_barrier_semaphore()
    peers = [sibling, across] + x_peers + z_peers + y_peers
    for peer in peers:
        pl.semaphore_signal(barrier, inc=1, device_id=peer, device_id_type=MESH)
    pl.semaphore_wait(barrier, len(peers))

    def weights(b):
        @pl.loop(0, ROWS // K)
        def _(i):
            lanes = pl.ds(pl.multiple_of(i * K, K), K)
            both = wt[b, :, :, :, lanes].reshape(K, K)
            wh[b, :, lanes], wl[b, :, lanes] = split(both)

    def project(b, start):
        at = pl.ds(start, HALF)
        pt[b, at, :] = dot3(zh[at, :], zl[at, :], wh[b], wl[b], NT)

    def update(b, start):
        at = pl.ds(start, HALF)
        s_high, s_low = split(st[b, at, :])
        for i in range(ROWS // K):
            lanes = pl.ds(i * K, K)
            fresh = zt[at, lanes] - dot3(s_high, s_low, wh[b, :, lanes], wl[b, :, lanes], NN)
            zt[at, lanes] = fresh
            if b == APPLIED:
                zh[at, lanes], zl[at, lanes] = split(fresh)

    def store(start, sem):
        at = pl.ds(start, HALF)
        copy = pltpu.make_async_copy(zt.at[at], out_ref.at[at], sem)
        copy.start()
        stores.append(copy)

    stores = []
    gathered = [None] * len(UNITS)

    def z_flow(u):
        b, h, at, rows = UNITS[u]
        lanes = pl.ds(at, rows)
        gathered[u] = [
            send(
                w_ref.at[b, h, :, lanes], wt.at[b, col, h, :, lanes],
                zg_s.at[u, d], zg_r.at[u, d], z_peers[d],
            )
            for d in range(3)
        ]
        yield

    def y_flow(u):
        b, h, at, rows = UNITS[u]
        lanes = pl.ds(at, rows)
        if u == FIRST[b]:
            fetch_w[b].wait()
        received(gathered[u])
        run = wt.at[b, pl.ds(4 * y, 4), h, :, lanes]
        up, down = [
            send(run, run, yg_s.at[u, d], yg_r.at[u, d], y_peers[d]) for d in range(2)
        ]
        yield
        up.wait_recv()
        part = wt.at[b, pl.ds(4 * y_down, 2), h, :, lanes]
        one = send(part, part, fg_s.at[u, 0], fg_r.at[u, 0], y_peers[0])
        down.wait_recv()
        part = wt.at[b, pl.ds(4 * y_up + 2, 2), h, :, lanes]
        two = send(part, part, fg_s.at[u, 1], fg_r.at[u, 1], y_peers[1])
        yield
        received([one, two])
        if u == LAST[b]:
            weights(b)
        yield

    def c_flow(b):
        cp[b] = dot3(wh[b, PANEL:, :], wl[b, PANEL:, :], wh[b, :PANEL, :], wl[b, :PANEL, :], NT)
        to_core = send(cp.at[b, c_theirs], cc.at[b], cc_s.at[b], cc_r.at[b], sibling)
        yield
        to_core.wait_recv()
        cp[b, c_mine, :] = cp[b, c_mine, :] + cc[b]
        to_x = [
            send(cp.at[b, c_mine], cx.at[b, d], cx_s.at[b, d], cx_r.at[b, d], x_peers[d])
            for d in range(3)
        ]
        yield
        received(to_x)
        cs[b] = (cp[b, c_mine, :] + cx[b, 0]) + (cx[b, 1] + cx[b, 2])
        to_z = send(cs.at[b], cz.at[b], cz_s.at[b], cz_r.at[b], across)
        yield
        to_z.wait_recv()
        cf[b, c_mine, :] = cs[b] + cz[b]
        part = cf.at[b, c_mine]
        to_core = send(part, part, cf_s.at[b], cf_r.at[b], sibling)
        yield
        to_core.wait_recv()
        yield

    def p_flow(b):
        project(b, theirs)
        to_core = send(
            pt.at[b, pl.ds(theirs, HALF)], rc.at[b], pc_s.at[b], pc_r.at[b], sibling
        )
        yield
        project(b, mine)
        yield
        to_core.wait_recv()
        at = pl.ds(mine, HALF)
        pt[b, at, :] = pt[b, at, :] + rc[b]
        to_x = []
        for d in range(3):
            to = pl.multiple_of(mine + ((x + 1 + d) % 4) * PIECE, PIECE)
            to_x.append(
                send(
                    pt.at[b, pl.ds(to, PIECE)], rx.at[b, d],
                    px_s.at[b, d], px_r.at[b, d], x_peers[d],
                )
            )
        yield
        received(to_x)
        ps[b] = (pt[b, piece_rows, :] + rx[b, 0]) + (rx[b, 1] + rx[b, 2])
        to_z = send(ps.at[b], rz.at[b], pz_s.at[b], pz_r.at[b], across)
        yield
        to_z.wait_recv()
        yield

    def g_flow(b):
        g, wide = b - 1, len(PAIRS[b]) * K
        own = wt[b, pl.ds(4 * y, 4)].reshape(RUN, ROWS)
        own_high, own_low = split(own)
        for i, c in enumerate(PAIRS[b]):
            gp[g, :, i * K : (i + 1) * K] = dot3(own_high, own_low, wh[c], wl[c], NT)
        lanes = pl.ds(0, wide)
        base = pl.multiple_of(core * 32, 32)
        other = pl.multiple_of((1 - core) * 32, 32)
        to_core = send(
            gp.at[g, pl.ds(other, 32), lanes], gc.at[g, :, lanes], gc_s.at[g], gc_r.at[g], sibling
        )
        yield
        to_core.wait_recv()
        at = pl.ds(base, 32)
        gp[g, at, :wide] = gp[g, at, :wide] + gc[g, :, :wide]
        to_x = []
        for d in range(3):
            to = pl.multiple_of(base + ((x + 1 + d) % 4) * 8, 8)
            to_x.append(
                send(
                    gp.at[g, pl.ds(to, 8), lanes], gx.at[g, d, :, lanes],
                    gx_s.at[g, d], gx_r.at[g, d], x_peers[d],
                )
            )
        yield
        received(to_x)
        at = pl.ds(pl.multiple_of(base + x * 8, 8), 8)
        gs[g, :, :wide] = (gp[g, at, :wide] + gx[g, 0, :, :wide]) + (
            gx[g, 1, :, :wide] + gx[g, 2, :, :wide]
        )
        to_z = send(
            gs.at[g, :, lanes], gz.at[g, :, lanes], gz_s.at[g], gz_r.at[g], across
        )
        yield
        to_z.wait_recv()
        gt[g, y, core, x, :, :wide] = gs[g, :, :wide] + gz[g, :, :wide]
        part = gt.at[g, y, core, x, :, lanes]
        up, down = [
            send(part, part, gy_s.at[g, d], gy_r.at[g, d], y_peers[d]) for d in range(2)
        ]
        yield
        up.wait_recv()
        part = gt.at[g, y_down, core, x, :, pl.ds(0, wide // 2)]
        one = send(part, part, gf_s.at[g, 0], gf_r.at[g, 0], y_peers[0])
        down.wait_recv()
        part = gt.at[g, y_up, core, x, :, pl.ds(wide // 2, wide // 2)]
        two = send(part, part, gf_s.at[g, 1], gf_r.at[g, 1], y_peers[1])
        yield
        received([one, two])
        part = gt.at[g, :, core, x, :, lanes]
        to_x = [
            send(part, part, ga_s.at[g, d], ga_r.at[g, d], x_peers[d]) for d in range(3)
        ]
        yield
        received(to_x)
        part = gt.at[g, :, core, :, :, lanes]
        to_core = send(part, part, ge_s.at[g], ge_r.at[g], sibling)
        yield
        to_core.wait_recv()
        total = None
        for i, c in enumerate(PAIRS[b]):
            seen = gt[g, :, :, :, :, i * K : (i + 1) * K].reshape(K, K)
            term = exact(st[c, piece_rows, :], seen, NT)
            total = term if total is None else total + term
        fix[g] = total
        yield

    def s_flow(b):
        total = ps[b] + rz[b]
        if b:
            total = total - fix[b - 1]
        tail = exact(total[:, PANEL:], tf[b, 1], NT)
        lead = exact(total[:, :PANEL] - exact(tail, cf[b], NN), tf[b, 0], NT)
        st[b, piece_rows, :PANEL] = lead
        st[b, piece_rows, PANEL:] = tail
        part = st.at[b, piece_rows]
        to_x = [
            send(part, part, sx_s.at[b, d], sx_r.at[b, d], x_peers[d]) for d in range(3)
        ]
        to_core = [send(part, part, sc_s.at[b, 3], sc_r.at[b, 3], sibling)]
        yield
        for d in range(3):
            to_x[d].wait_recv()
            at = pl.multiple_of(mine + ((x + 3 - d) % 4) * PIECE, PIECE)
            part = st.at[b, pl.ds(at, PIECE)]
            to_core.append(send(part, part, sc_s.at[b, d], sc_r.at[b, d], sibling))
        if b == BLOCKS - 1:
            update(b, mine)
            store(mine, local_sem.at[0])
        yield
        received(to_core)
        if b < BLOCKS - 1:
            update(b, mine)
        update(b, theirs)
        if b == BLOCKS - 1:
            store(theirs, local_sem.at[1])
        yield

    def start(_):
        fetch_t.wait()
        fetch_z.wait()

        @pl.loop(0, ROWS // 128)
        def _(i):
            at = pl.ds(pl.multiple_of(i * 128, 128), 128)
            turned = zs[at, :].T
            zt[:, at] = turned
            zh[:, at], zl[:, at] = split(turned)

        yield

    flows = {"t": start, "z": z_flow, "y": y_flow, "c": c_flow, "p": p_flow, "g": g_flow, "s": s_flow}
    steps = {}
    for name in ORDER:
        if name not in steps:
            steps[name] = flows[name[0]](int(name[1:]))
        next(steps[name])

    for copy in sent:
        copy.wait_send()
    for copy in stores:
        copy.wait()


def per_device(eigvec, householder, panel_factors):
    dma = pltpu.SemaphoreType.DMA
    n, g = BLOCKS, BLOCKS - 1
    scratch = [
        pltpu.VMEM((ROWS, COLS), F32),
        pltpu.VMEM((COLS, ROWS), F32),
        pltpu.VMEM((COLS, ROWS), BF16),
        pltpu.VMEM((COLS, ROWS), BF16),
        pltpu.VMEM((n, 16, 2, 8, ROWS), F32),
        pltpu.VMEM((n, K, ROWS), BF16),
        pltpu.VMEM((n, K, ROWS), BF16),
        pltpu.VMEM((n, 2, PANEL, PANEL), F32),
        pltpu.VMEM((n, COLS, K), F32),
        pltpu.VMEM((n, HALF, K), F32),
        pltpu.VMEM((n, 3, PIECE, K), F32),
        pltpu.VMEM((n, PIECE, K), F32),
        pltpu.VMEM((n, PIECE, K), F32),
        pltpu.VMEM((n, PANEL, PANEL), F32),
        pltpu.VMEM((n, C_HALF, PANEL), F32),
        pltpu.VMEM((n, 3, C_HALF, PANEL), F32),
        pltpu.VMEM((n, C_HALF, PANEL), F32),
        pltpu.VMEM((n, C_HALF, PANEL), F32),
        pltpu.VMEM((n, PANEL, PANEL), F32),
        pltpu.VMEM((g, RUN, WIDE), F32),
        pltpu.VMEM((g, RUN // 2, WIDE), F32),
        pltpu.VMEM((g, 3, 8, WIDE), F32),
        pltpu.VMEM((g, 8, WIDE), F32),
        pltpu.VMEM((g, 8, WIDE), F32),
        pltpu.VMEM((g, 4, 2, 4, 8, WIDE), F32),
        pltpu.VMEM((g, PIECE, K), F32),
        pltpu.VMEM((n, COLS, K), F32),
        dma((2 + n,)),
    ]
    for shape in (
        (len(UNITS), 3), (len(UNITS), 2), (len(UNITS), 2),
        (n,), (n, 3), (n,),
        (n,), (n, 3), (n,), (n,),
        (g,), (g, 3), (g,), (g, 2), (g, 2), (g, 3), (g,),
        (n, 3), (n, 4),
    ):
        scratch += [dma(shape), dma(shape)]
    turned = pl.pallas_call(
        kernel,
        out_shape=jax.ShapeDtypeStruct((COLS, ROWS), F32),
        in_specs=[pl.BlockSpec(memory_space=pl.ANY)] * 3,
        out_specs=pl.BlockSpec(memory_space=pl.ANY),
        scratch_shapes=scratch,
        compiler_params=pltpu.CompilerParams(
            collective_id=0, has_side_effects=True, vmem_limit_bytes=58 << 20
        ),
        cost_estimate=pl.CostEstimate(
            flops=2 * 2 * 3 * n * K * ROWS * COLS, bytes_accessed=8 << 20, transcendentals=0
        ),
        name="back_transform",
    )(
        eigvec,
        jnp.transpose(householder, (0, 2, 1)).reshape(n, 2, 8, ROWS),
        panel_factors,
    )
    return turned.T


def solution(mesh):
    in_specs = (P("row", "col"), P(None, "row", "col"), P())
    out_specs = P("row", "col")
    return jax.shard_map(
        per_device, mesh=mesh, in_specs=in_specs, out_specs=out_specs, check_vma=False
    )
```
